32 devices in a mesh: lev: 4 (over x, core), tile: 8 (over z, y).
Axes of the slice: x: 2, y: 2, z: 4, core: 2. Of those that a mesh axis runs over, the one named last changes fastest.
Arguments:
- forcing: bfloat16 [4, 8, 36, 36, 128], P('lev', 'tile'), may hold values from -6 to 6
- transport: float32 [4, 4, 8, 36, 36], P(None, 'lev', 'tile'), may hold values from 0.04 to 0.22
- reactivity: float32 [4, 8, 36, 36], P('lev', 'tile'), may hold values from 0.1 to 0.6
- jacobian: float32 [4, 128, 128], P('lev'), may hold values from -0.5 to 0.5
- pattern: int32 [8, 8], replicated, may hold values 0 or 1
- lon_rate: float32 [128, 36], P('tile'), may hold values from 0.003 to 0.03
- lat_rate: float32 [128, 288], P('tile'), may hold values from 0.003 to 0.03
- vertical: float32 [128, 4, 4], replicated, may hold values from -3 to 3
- step_scale: float32 [128], replicated, may hold values from 0.3 to 1
- control: bfloat16 [4, 8, 36, 36, 128], P('lev', 'tile'), may hold values from -6 to 6
Outputs:
- control_new: bfloat16 [4, 8, 36, 36, 128], P('lev', 'tile')
The draws below stay inside these ranges and needn't reach their ends.
All inputs are finite; a program needn't handle non-finite values.
Results may differ from the reference program's by a relative error of at most 0.001.
The reference program's roundings to bfloat16 on the way (of `gradient` and `filtered`) count: a program that leaves them out, or rounds other values in their place, can miss the bound.
Values may be sent and summed in bfloat16 or wider, within the bound.
A program may use at most 64 MiB of HBM per device.

```python
import math
import jax
import jax.numpy as jnp
from jax import lax

S = 128
TJ = 8
STEPS = 3
TX = 36
TY = 36
LEV = 4
TILES = 8
NLON = 36
NLAT = 288
NBLK = 8


def with_ends(array, stream_key, least, largest):
    index_at = [jax.random.randint(jax.random.fold_in(stream_key, axis), (), 0, length) for axis, length in enumerate(array.shape)]
    main_axis = array.shape.index(max(array.shape))
    neighbour = index_at[:main_axis] + [(index_at[main_axis] + 1) % array.shape[main_axis]] + index_at[main_axis + 1:]
    return array.at[tuple(index_at)].set(least).at[tuple(neighbour)].set(largest)


def level_of(rng, dims, shards, smallest, largest):
    factor_of, own = 1.0, jax.random.fold_in(rng, 6)
    for dim, parts in shards:
        draws = jnp.exp(jax.random.uniform(jax.random.fold_in(own, dim), (parts,), jnp.float32, smallest / len(shards), largest / len(shards)))
        factor_of = factor_of * jnp.repeat(draws, dims[dim] // parts).reshape([-1 if axis == dim else 1 for axis in range(len(dims))])
    return factor_of


def gaussian(key, shape, deviation, reach, pieces=(), held_as=jnp.bfloat16):
    drawn = deviation * jax.random.normal(key, shape, jnp.float32)
    if pieces:
        drawn = drawn * level_of(key, shape, pieces, -0.22, 0.18)
    return jnp.clip(drawn, -reach, reach).astype(held_as)


def setup_inputs(seed: int = 0) -> dict:
    key_list = jax.random.split(jax.random.key(seed), 11)
    forcing = gaussian(key_list[0], (LEV, TILES, TX, TY, S), 1.0, 6.0, ((0, 4), (1, 8)))
    transport = jnp.clip(0.04 + 0.18 * jax.random.uniform(key_list[1], (4, LEV, TILES, TX, TY), jnp.float32) ** level_of(key_list[1], (4, LEV, TILES, TX, TY), ((1, 4), (2, 8)), -0.2, 0.2), 0.04, 0.22)
    reactivity = jnp.clip(jnp.exp(math.log(0.6) - 1.7917595 * jax.random.uniform(key_list[2], (LEV, TILES, TX, TY), jnp.float32) ** level_of(key_list[2], (LEV, TILES, TX, TY), ((0, 4), (1, 8)), -0.2, 0.2)), 0.1, 0.6)
    jacobian = gaussian(key_list[3], (LEV, S, S), S ** -0.5, 0.5, ((0, 4),), jnp.float32)
    pattern = with_ends((jax.random.randint(key_list[4], (NBLK, NBLK), 0, 2) < 1).astype(jnp.int32), jax.random.fold_in(key_list[4], 1), 0, 1)
    lon_rate = jnp.clip(jnp.exp(math.log(0.03) - 2.3025851 * jax.random.uniform(key_list[5], (S, NLON), jnp.float32) ** level_of(key_list[5], (S, NLON), ((0, 8),), -0.2, 0.2)), 0.003, 0.03)
    lat_rate = jnp.clip(jnp.exp(math.log(0.03) - 2.3025851 * jax.random.uniform(key_list[6], (S, NLAT), jnp.float32) ** level_of(key_list[6], (S, NLAT), ((0, 8),), -0.2, 0.2)), 0.003, 0.03)
    vertical = gaussian(key_list[7], (S, LEV, LEV), 0.5, 3.0, (), jnp.float32)
    step_scale = jnp.clip(jnp.exp(jax.random.uniform(key_list[8], (S,), jnp.float32, math.log(0.3), math.log(1.0))), 0.3, 1.0)
    control = gaussian(key_list[9], (LEV, TILES, TX, TY, S), 1.0, 6.0, ((0, 4), (1, 8)))
    return {"forcing": forcing, "transport": transport, "reactivity": reactivity, "jacobian": jacobian, "pattern": pattern, "lon_rate": lon_rate, "lat_rate": lat_rate, "vertical": vertical, "step_scale": step_scale, "control": control}


def to_grid(values):
    lon_tiles = values.shape[0] // TJ
    shaped = values.reshape((lon_tiles, TJ) + values.shape[1:])
    shaped = jnp.swapaxes(shaped, 1, 2)
    return shaped.reshape((lon_tiles * values.shape[1], TJ * values.shape[2]) + values.shape[3:])

def to_tiles(values, tile_rows, tile_cols):
    lon_tiles = values.shape[0] // tile_rows
    shaped = values.reshape((lon_tiles, tile_rows, TJ, tile_cols) + values.shape[2:])
    shaped = jnp.swapaxes(shaped, 1, 2)
    return shaped.reshape((lon_tiles * TJ, tile_rows, tile_cols) + values.shape[2:])

def exp_filter(values, rates):
    rates_line = rates.T
    quarter = jnp.sqrt(jnp.sqrt(rates_line))
    scaled = values * quarter[:, None, :]
    decay = jnp.exp(-rates_line)
    decay_after = jnp.concatenate([decay[1:], jnp.zeros_like(decay[:1])], 0)

    def forward(carry, inputs):
        item, factor = inputs
        carry = item + factor[None, :] * carry
        return (carry, carry)
    anchor = jnp.zeros(values.shape[1:], values.dtype)
    _, ahead = lax.scan(forward, anchor, (scaled, decay))
    _, behind = lax.scan(forward, anchor, (scaled, decay_after), reverse=True)
    return quarter[:, None, :] * (ahead + behind - scaled)

def reference(forcing, transport, reactivity, jacobian, pattern, lon_rate, lat_rate, vertical, step_scale, control):
    groups = pattern.shape[0]
    width = S // groups
    blockmask = jnp.broadcast_to(pattern.astype(jnp.float32)[:, None, :, None], (groups, width, groups, width)).reshape(S, S)

    def one_level(inputs):
        forcing_level, transport_level, reactivity_level, jacobian_level = inputs
        adjoint = to_grid(forcing_level).astype(jnp.float32)
        weights = [to_grid(transport_level[k])[:, :, None] for k in range(4)]
        reacting = to_grid(reactivity_level)[:, :, None]
        coupling = jacobian_level * blockmask
        for sweep in range(STEPS):
            from_west = jnp.roll(adjoint, 1, axis=0)
            from_east = jnp.roll(adjoint, -1, axis=0)
            zero_column = jnp.zeros_like(adjoint[:, :1])
            from_south = jnp.concatenate([zero_column, adjoint[:, :-1]], 1)
            from_north = jnp.concatenate([adjoint[:, 1:], zero_column], 1)
            moved = adjoint + weights[0] * (from_west - adjoint) + weights[1] * (from_east - adjoint) + weights[2] * (from_south - adjoint) + weights[3] * (from_north - adjoint)
            reacted = jnp.dot(moved.reshape(-1, S), coupling, precision=lax.Precision.HIGHEST, preferred_element_type=jnp.float32)
            adjoint = moved + reacting * reacted.reshape(moved.shape)
        gradient = lax.optimization_barrier(adjoint.astype(jnp.bfloat16)).astype(jnp.float32)
        along_lon = exp_filter(gradient, lon_rate)
        along_lat = exp_filter(jnp.swapaxes(along_lon, 0, 1), lat_rate)
        filtered = jnp.swapaxes(along_lat, 0, 1).astype(jnp.bfloat16)
        return to_tiles(filtered, TX, TY)
    filtered_all = lax.map(one_level, (forcing, jnp.moveaxis(transport, 1, 0), reactivity, jacobian))

    def update_level(inputs):
        level, control_level = inputs
        mixing = vertical[:, level, :]
        total = jnp.zeros(control_level.shape, jnp.float32)
        for other in range(LEV):
            total = total + mixing[:, other] * filtered_all[other].astype(jnp.float32)
        return (control_level.astype(jnp.float32) - step_scale * total).astype(jnp.bfloat16)
    return lax.map(update_level, (jnp.arange(LEV, dtype=jnp.int32), control))
```

```python
import functools

import jax
import jax.numpy as jnp
from jax import lax
from jax.experimental import pallas as pl
from jax.experimental.pallas import tpu as pltpu
from jax.sharding import PartitionSpec as P

TJ = 8
STEPS = 3


HIGHEST = lax.Precision.HIGHEST


def from_behind(x, axis, by):
    size = lax.axis_size(axis)
    return lax.ppermute(x, axis, [(i, (i + by) % size) for i in range(size)])


def neighbour_rim(edge, offset):
    return from_behind(edge, "tile", offset)


def filter_kernel(rates, blocks):
    cumulative = jnp.cumsum(rates)
    quarter = jnp.sqrt(jnp.sqrt(rates))
    kernel = (
        quarter[:, None]
        * quarter[None, :]
        * jnp.exp(-jnp.abs(cumulative[:, None] - cumulative[None, :]))
    )
    length = rates.shape[0] // blocks
    return kernel.reshape(blocks, length, blocks, length)


def on_device_general(
    forcing,
    transport,
    reactivity,
    jacobian,
    pattern,
    lon_rate,
    lat_rate,
    vertical,
    step_scale,
    control,
):
    adjoint = forcing[0, 0].astype(jnp.float32)
    tile_rows, tile_cols, species = adjoint.shape
    weights = transport[:, 0, 0]
    reacting = reactivity[0, 0][:, :, None]
    groups = pattern.shape[0]
    width = species // groups
    blockmask = jnp.broadcast_to(
        pattern.astype(jnp.float32)[:, None, :, None], (groups, width, groups, width)
    ).reshape(species, species)
    coupling = jacobian[0] * blockmask
    tiles = lax.axis_size("tile")
    lon_tiles = tiles // TJ
    placing = lax.axis_index("tile") % TJ
    keep_south = (placing > 0).astype(jnp.float32)
    keep_north = (placing < TJ - 1).astype(jnp.float32)
    for sweep in range(STEPS):
        if lon_tiles > 1:
            west_rim = neighbour_rim(adjoint[-1], TJ)
            east_rim = neighbour_rim(adjoint[0], -TJ)
        else:
            west_rim = adjoint[-1]
            east_rim = adjoint[0]
        south_rim = neighbour_rim(adjoint[:, -1], 1) * keep_south
        north_rim = neighbour_rim(adjoint[:, 0], -1) * keep_north
        from_west = jnp.concatenate([west_rim[None], adjoint[:-1]], 0)
        from_east = jnp.concatenate([adjoint[1:], east_rim[None]], 0)
        from_south = jnp.concatenate([south_rim[:, None], adjoint[:, :-1]], 1)
        from_north = jnp.concatenate([adjoint[:, 1:], north_rim[:, None]], 1)
        moved = (
            adjoint
            + weights[0][:, :, None] * (from_west - adjoint)
            + weights[1][:, :, None] * (from_east - adjoint)
            + weights[2][:, :, None] * (from_south - adjoint)
            + weights[3][:, :, None] * (from_north - adjoint)
        )
        reacted = jnp.dot(
            moved.reshape(tile_rows * tile_cols, species),
            coupling,
            precision=HIGHEST,
            preferred_element_type=jnp.float32,
        )
        adjoint = moved + reacting * reacted.reshape(tile_rows, tile_cols, species)
    gradient = adjoint.astype(jnp.bfloat16)
    planes = lax.all_to_all(
        gradient.reshape(1, tile_rows * tile_cols, species),
        "tile",
        split_axis=2,
        concat_axis=0,
        tiled=True,
    )
    owned = planes.shape[2]
    planes = jnp.moveaxis(planes.reshape(lon_tiles, TJ, tile_rows, tile_cols, owned), 4, 0)

    def filter_species(inputs):
        lon_line, lat_line, plane = inputs
        lon_kernel = filter_kernel(lon_line, lon_tiles)
        lat_kernel = filter_kernel(lat_line, TJ)
        along_lon = jnp.einsum(
            "abcd,cjdy->ajby", lon_kernel, plane.astype(jnp.float32), precision=HIGHEST
        )
        return jnp.einsum("jykz,akbz->ajby", lat_kernel, along_lon, precision=HIGHEST).astype(
            jnp.bfloat16
        )

    filtered = jnp.moveaxis(lax.map(filter_species, (lon_rate, lat_rate, planes)), 0, 4)
    level_here = lax.axis_index("lev")
    mixing = lax.dynamic_index_in_dim(vertical, level_here, 1, keepdims=False)
    returned = lax.all_to_all(
        filtered.reshape(tiles, tile_rows * tile_cols, owned),
        "tile",
        split_axis=0,
        concat_axis=2,
        tiled=True,
    )
    factor = mixing.T
    summed = jnp.sum(
        lax.all_gather(returned, "lev", axis=0, tiled=True) * factor[:, None, :], axis=0
    )
    increment = summed.reshape(tile_rows, tile_cols, species)
    updated = control[0, 0].astype(jnp.float32) - step_scale * increment
    return updated.astype(jnp.bfloat16)[None, None]


MESH = pl.DeviceIdType.MESH
RIM = STEPS
CHUNK = 10
PIECES = 6


def up_to(size, multiple):
    return -(-size // multiple) * multiple


def fused_kernel(
    tiles,
    levels,
    forcing_ref,
    transport_ref,
    reactivity_ref,
    jacobian_ref,
    pattern_ref,
    lon_rate_ref,
    lat_rate_ref,
    vertical_ref,
    step_scale_ref,
    control_ref,
    out_ref,
    state_a,
    state_b,
    weights_own,
    weights_rim,
    weights,
    moved_ref,
    split_ref,
    plane,
    ahead_ref,
    rates_own,
    rates_all,
    carry_out,
    carry_in,
    fields,
    halo_send,
    halo_recv,
    rim_send,
    rim_recv,
    rate_send,
    rate_recv,
    carry_send,
    carry_recv,
    level_send,
    level_recv,
):
    nlon, nlat, species = forcing_ref.shape
    pitch = state_a.shape[1]
    rows = nlat + 2 * RIM
    owned, lat_total = lat_rate_ref.shape
    lon_at = up_to(lat_total, 128)
    rate_width = rates_own.shape[1]
    t = lax.axis_index("tile")
    level = lax.axis_index("lev")
    sibling = level + 1 - 2 * lax.rem(level, 2)
    across = lax.rem(level + 2, levels)
    f32, bf16 = jnp.float32, jnp.bfloat16

    barrier = pltpu.get_barrier_semaphore()
    for o in range(1, tiles):
        pl.semaphore_signal(
            barrier, inc=1, device_id=(level, lax.rem(t + o, tiles)), device_id_type=MESH
        )
    for other in (sibling, across):
        pl.semaphore_signal(barrier, inc=1, device_id=(other, t), device_id_type=MESH)

    weights_own[...] = jnp.zeros_like(weights_own)
    weights_own[0:4, 0:nlon, 0:nlat] = transport_ref[...]
    weights_own[4, 0:nlon, 0:nlat] = reactivity_ref[...]
    rates_own[...] = jnp.zeros_like(rates_own)
    rates_own[:, 0:lat_total] = lat_rate_ref[...]
    rates_own[:, lon_at : lon_at + nlon] = lon_rate_ref[...]
    plane[...] = jnp.zeros_like(plane)
    for i in range(nlon):
        plane[i * pitch : i * pitch + nlat, :] = forcing_ref[i].astype(f32)
    plane[nlon * pitch : nlon * pitch + nlat, :] = forcing_ref[0].astype(f32)
    plane[(pitch - 1) * pitch : (pitch - 1) * pitch + nlat, :] = forcing_ref[nlon - 1].astype(f32)
    for j in range(nlat):
        state_a[RIM + j] = plane[pl.ds(j, pitch, stride=pitch), :]

    pl.semaphore_wait(barrier, tiles + 1)

    def halo(side):
        if side == 0:
            source, target, place = pl.ds(nlat, RIM), pl.ds(0, RIM), t + 1
        else:
            source, target, place = pl.ds(RIM, RIM), pl.ds(nlat + RIM, RIM), t - 1
        return (
            pltpu.make_async_remote_copy(
                src_ref=state_a.at[source],
                dst_ref=state_a.at[target],
                send_sem=halo_send.at[side],
                recv_sem=halo_recv.at[side],
                device_id=(level, place),
                device_id_type=MESH,
            ),
            pltpu.make_async_remote_copy(
                src_ref=weights_own,
                dst_ref=weights_rim.at[side],
                send_sem=rim_send.at[side],
                recv_sem=rim_recv.at[side],
                device_id=(level, place),
                device_id_type=MESH,
            ),
        )

    sends = [halo(0), halo(1)]

    @pl.when(t < tiles - 1)
    def _():
        for copy in sends[0]:
            copy.start()

    @pl.when(t > 0)
    def _():
        for copy in sends[1]:
            copy.start()

    @pl.when(t == 0)
    def _():
        state_a[0:RIM] = jnp.zeros((RIM, pitch, species), f32)
        weights_rim[0] = jnp.zeros(weights_rim.shape[1:], f32)

    @pl.when(t == tiles - 1)
    def _():
        state_a[nlat + RIM : rows] = jnp.zeros((RIM, pitch, species), f32)
        weights_rim[1] = jnp.zeros(weights_rim.shape[1:], f32)

    mine = pl.ds(pl.multiple_of(t * owned, owned), owned)
    rate_copies = []
    for o in range(1, tiles):
        rate_copies.append(
            pltpu.make_async_remote_copy(
                src_ref=rates_own,
                dst_ref=rates_all.at[mine],
                send_sem=rate_send.at[o - 1],
                recv_sem=rate_recv.at[o - 1],
                device_id=(level, lax.rem(t + o, tiles)),
                device_id_type=MESH,
            )
        )
        rate_copies[-1].start()
    rates_all[mine, :] = rates_own[...]

    for j in range(nlat):
        weights[:, RIM + j] = jnp.broadcast_to(
            weights_own[:, :, j : j + 1], (5, pitch, species)
        )

    groups = pattern_ref.shape[0]
    width = species // groups
    member = (
        lax.broadcasted_iota(jnp.int32, (species, groups), 0) // width
        == lax.broadcasted_iota(jnp.int32, (species, groups), 1)
    ).astype(f32)
    mask = lax.dot_general(
        jnp.dot(member, pattern_ref[...].astype(f32), preferred_element_type=f32),
        member,
        (((1,), (1,)), ((), ())),
        preferred_element_type=f32,
    )
    coupling = jacobian_ref[...] * mask
    high = coupling.astype(bf16)
    low = (coupling - high.astype(f32)).astype(bf16)
    both = jnp.concatenate(
        [
            jnp.concatenate([high, low], 1),
            jnp.concatenate([high, jnp.zeros_like(low)], 1),
        ],
        0,
    )

    @pl.when(t > 0)
    def _():
        sends[0][0].wait_recv()
        sends[0][1].wait_recv()

    @pl.when(t < tiles - 1)
    def _():
        sends[1][0].wait_recv()
        sends[1][1].wait_recv()

    for r in range(1, RIM):
        weights[:, r] = jnp.broadcast_to(
            weights_rim[0, :, :, nlat - RIM + r : nlat - RIM + r + 1], (5, pitch, species)
        )
        weights[:, nlat + RIM + r - 1] = jnp.broadcast_to(
            weights_rim[1, :, :, r - 1 : r], (5, pitch, species)
        )

    @pl.when(t < tiles - 1)
    def _():
        sends[0][0].wait_send()
        sends[0][1].wait_send()

    @pl.when(t > 0)
    def _():
        sends[1][0].wait_send()
        sends[1][1].wait_send()

    def step(source, target, first, last, final):
        for j0 in range(first, last, CHUNK):
            n = min(CHUNK, last - j0)
            for j in range(j0, j0 + n, 2):
                here = source[j : j + 2]
                moved = (
                    here
                    + weights[0, j : j + 2] * (pltpu.roll(here, 1, 1) - here)
                    + weights[1, j : j + 2] * (pltpu.roll(here, pitch - 1, 1) - here)
                    + weights[2, j : j + 2] * (source[j - 1 : j + 1] - here)
                    + weights[3, j : j + 2] * (source[j + 1 : j + 3] - here)
                )
                moved = moved.reshape(2 * pitch, species)
                at = pl.ds((j - first) * pitch, 2 * pitch)
                moved_ref[at, :] = moved
                top = moved.astype(bf16)
                split_ref[at, 0:species] = top
                split_ref[at, species:] = (moved - top.astype(f32)).astype(bf16)
            at = pl.ds((j0 - first) * pitch, n * pitch)
            product = jnp.dot(split_ref[at, :], both, preferred_element_type=f32)
            reacted = product[:, :species] + product[:, species:]
            after = moved_ref[at, :].reshape(n, pitch, species) + weights[
                4, j0 : j0 + n
            ] * reacted.reshape(n, pitch, species)
            if final:
                target[j0 : j0 + n] = after.astype(bf16).astype(f32)
            else:
                target[j0 : j0 + n] = after
                target[j0 : j0 + n, nlon : nlon + 1] = after[:, 0:1]
                target[j0 : j0 + n, pitch - 1 : pitch] = after[:, nlon - 1 : nlon]

    states = [state_a, state_b]
    for sweep in range(STEPS):
        step(
            states[sweep % 2],
            states[(sweep + 1) % 2],
            1 + sweep,
            rows - 1 - sweep,
            sweep == STEPS - 1,
        )
    gradient = states[STEPS % 2]

    for copy in rate_copies:
        copy.wait()
    cell = lax.broadcasted_iota(jnp.int32, (pitch, rate_width), 1)
    row = lax.broadcasted_iota(jnp.int32, (pitch, rate_width), 0)
    start = t * nlat
    lat_cell = cell < lat_total
    picks = jnp.concatenate(
        [
            (cell == start + row) & (row < nlat),
            (cell >= start) & (cell <= start + row) & (cell < start + nlat),
            (cell < row * nlat) & lat_cell,
            (cell == lon_at + row) & (row < nlon),
        ],
        0,
    ).astype(f32)
    lines = lax.dot_general(
        picks,
        rates_all[...],
        (((1,), (1,)), ((), ())),
        precision=HIGHEST,
        preferred_element_type=f32,
    )
    lat_line = lines[0:pitch]
    lat_sum = lines[pitch : 2 * pitch]
    before = lines[2 * pitch : 3 * pitch]
    lon_line = lines[3 * pitch :]
    lat_q, lat_d = jnp.sqrt(jnp.sqrt(lat_line)), jnp.exp(-lat_line)
    lon_q, lon_d = jnp.sqrt(jnp.sqrt(lon_line)), jnp.exp(-lon_line)
    from_south = lat_q * jnp.exp(-lat_sum)
    from_north = lat_q * jnp.exp(lat_sum - lat_sum[nlat - 1 : nlat])

    carry = jnp.zeros((pitch, species), f32)
    for j in range(nlat):
        carry = lat_q[j : j + 1] * gradient[RIM + j] + lat_d[j : j + 1] * carry
        ahead_ref[j] = carry
    carry_out[0] = carry
    carry = jnp.zeros((pitch, species), f32)
    for j in range(nlat - 1, -1, -1):
        item = lat_q[j : j + 1] * gradient[RIM + j]
        later = lat_d[j + 1 : j + 2] * carry if j < nlat - 1 else carry
        carry = item + later
        plane[j * pitch : (j + 1) * pitch, :] = lat_q[j : j + 1] * (ahead_ref[j] + later)
    carry_out[1] = lat_d[0:1] * carry

    carry_copies = []
    for o in range(1, tiles):
        carry_copies.append(
            pltpu.make_async_remote_copy(
                src_ref=carry_out.at[(t + o) // tiles],
                dst_ref=carry_in.at[o - 1],
                send_sem=carry_send.at[o - 1],
                recv_sem=carry_recv.at[o - 1],
                device_id=(level, lax.rem(t + o, tiles)),
                device_id_type=MESH,
            )
        )
        carry_copies[-1].start()

    order = lax.broadcasted_iota(jnp.int32, (pitch, species), 0)

    def before_tile(u):
        return jnp.sum(jnp.where(order == u, before, 0.0), 0, keepdims=True)

    south = jnp.zeros((pitch, species), f32)
    north = jnp.zeros((pitch, species), f32)
    for o in range(1, tiles):
        u = lax.rem(t + tiles - o, tiles)
        upper, lower = jnp.maximum(u, t), jnp.minimum(u, t)
        factor = jnp.exp(before_tile(lower + 1) - before_tile(upper))
        carry_copies[o - 1].wait()
        term = factor * carry_in[o - 1]
        south = south + jnp.where(o <= t, term, 0.0)
        north = north + jnp.where(o <= t, 0.0, term)
    for j in range(nlat):
        at = pl.ds(j * pitch, pitch)
        plane[at, :] = (
            plane[at, :] + from_south[j : j + 1] * south + from_north[j : j + 1] * north
        )

    carry = jnp.zeros((pitch, species), f32)
    for i in range(nlon):
        item = lon_q[i : i + 1] * plane[pl.ds(i, pitch, stride=pitch), :]
        carry = item + lon_d[i : i + 1] * carry
        ahead_ref[i] = carry

    def level_copy(source, target, k, place):
        return pltpu.make_async_remote_copy(
            src_ref=fields.at[source, k],
            dst_ref=fields.at[target, k],
            send_sem=level_send.at[target, k],
            recv_sem=level_recv.at[target, k],
            device_id=(place, t),
            device_id_type=MESH,
        )

    piece = nlon // PIECES
    carry = jnp.zeros((pitch, species), f32)
    far, near, relay = {}, {}, {}
    order_k = range(PIECES - 1, -1, -1)
    for k in order_k:
        for pair in range(piece // 2 - 1, -1, -1):
            done = []
            for i in (k * piece + 2 * pair + 1, k * piece + 2 * pair):
                item = lon_q[i : i + 1] * plane[pl.ds(i, pitch, stride=pitch), :]
                later = lon_d[i + 1 : i + 2] * carry if i < nlon - 1 else carry
                carry = item + later
                done.append(lon_q[i : i + 1] * (ahead_ref[i] + later))
            fields[0, k, 2 * pair * pitch : 2 * (pair + 1) * pitch, :] = jnp.concatenate(
                done[::-1], 0
            ).astype(bf16)
        far[k] = level_copy(0, 2, k, across)
        near[k] = level_copy(0, 1, k, sibling)
        far[k].start()
        near[k].start()

    factors = [
        vertical_ref[level, pl.ds(source, 1), :]
        for source in (level, sibling, across, lax.rem(sibling + 2, levels))
    ]
    scale = step_scale_ref[...]

    def finish(k):
        total = factors[0] * fields[0, k].astype(f32)
        for slot in range(1, levels):
            total = total + factors[slot] * fields[slot, k].astype(f32)
        total = (scale * total).reshape(piece, pitch, species)[:, :nlat]
        at = pl.ds(k * piece, piece)
        out_ref[at] = (control_ref[at].astype(f32) - total).astype(bf16)

    previous = None
    for k in order_k:
        far[k].wait_recv()
        relay[k] = level_copy(2, 3, k, sibling)
        relay[k].start()
        near[k].wait_recv()
        if previous is not None:
            relay[previous].wait_recv()
            finish(previous)
        previous = k
    relay[previous].wait_recv()
    finish(previous)
    for k in order_k:
        far[k].wait_send()
        near[k].wait_send()
        relay[k].wait_send()


def on_device_fused(
    tiles,
    levels,
    forcing,
    transport,
    reactivity,
    jacobian,
    pattern,
    lon_rate,
    lat_rate,
    vertical,
    step_scale,
    control,
):
    nlon, nlat, species = forcing.shape[2:]
    pitch = up_to(max(nlon + 2, nlat), 8)
    rows = nlat + 2 * RIM
    owned, lat_total = lat_rate.shape
    rate_width = up_to(lat_total, 128) + up_to(nlon, 128)
    f32, bf16 = jnp.float32, jnp.bfloat16
    dma = pltpu.SemaphoreType.DMA
    piece_rows = nlon // PIECES * pitch
    updated = pl.pallas_call(
        functools.partial(fused_kernel, tiles, levels),
        out_shape=jax.ShapeDtypeStruct((nlon, nlat, species), bf16),
        in_specs=[pl.BlockSpec(memory_space=pltpu.VMEM)] * 10,
        out_specs=pl.BlockSpec(memory_space=pltpu.VMEM),
        scratch_shapes=[
            pltpu.VMEM((rows, pitch, species), f32),
            pltpu.VMEM((rows, pitch, species), f32),
            pltpu.VMEM((5, pitch, 128), f32),
            pltpu.VMEM((2, 5, pitch, 128), f32),
            pltpu.VMEM((5, rows, pitch, species), f32),
            pltpu.VMEM((rows * pitch, species), f32),
            pltpu.VMEM((rows * pitch, 2 * species), bf16),
            pltpu.VMEM((pitch * pitch, species), f32),
            pltpu.VMEM((pitch, pitch, species), f32),
            pltpu.VMEM((owned, rate_width), f32),
            pltpu.VMEM((species, rate_width), f32),
            pltpu.VMEM((2, pitch, species), f32),
            pltpu.VMEM((tiles - 1, pitch, species), f32),
            pltpu.VMEM((levels, PIECES, piece_rows, species), bf16),
            dma((2,)),
            dma((2,)),
            dma((2,)),
            dma((2,)),
            dma((tiles - 1,)),
            dma((tiles - 1,)),
            dma((tiles - 1,)),
            dma((tiles - 1,)),
            dma((levels, PIECES)),
            dma((levels, PIECES)),
        ],
        compiler_params=pltpu.CompilerParams(
            collective_id=0, has_side_effects=True, vmem_limit_bytes=40 * 1024 * 1024
        ),
        name="fused",
    )(
        forcing[0, 0],
        transport[:, 0, 0],
        reactivity[0, 0],
        jacobian[0],
        pattern,
        lon_rate,
        lat_rate,
        jnp.transpose(vertical, (1, 2, 0)),
        step_scale[None],
        control[0, 0],
    )
    return updated[None, None]


def on_device(forcing, *others):
    tiles, levels = lax.axis_size("tile"), lax.axis_size("lev")
    nlon, nlat, species = forcing.shape[2:]
    one_ring = tiles == TJ and levels == 4
    fits = nlon % (2 * PIECES) == 0 and nlon == nlat and nlat % 2 == 0
    if one_ring and fits and species == 128:
        return on_device_fused(tiles, levels, forcing, *others)
    return on_device_general(forcing, *others)


def solution(mesh):
    in_specs = (
        P("lev", "tile", None, None, None),
        P(None, "lev", "tile", None, None),
        P("lev", "tile", None, None),
        P("lev", None, None),
        P(),
        P("tile", None),
        P("tile", None),
        P(),
        P(),
        P("lev", "tile", None, None, None),
    )
    out_specs = P("lev", "tile", None, None, None)
    return jax.shard_map(
        on_device, mesh=mesh, in_specs=in_specs, out_specs=out_specs, check_vma=False
    )
```

```python
import functools

import jax
import jax.numpy as jnp
from jax import lax
from jax.experimental import pallas as pl
from jax.experimental.pallas import tpu as pltpu
from jax.sharding import PartitionSpec as P

TJ = 8
STEPS = 3


HIGHEST = lax.Precision.HIGHEST


def from_behind(x, axis, by):
    size = lax.axis_size(axis)
    return lax.ppermute(x, axis, [(i, (i + by) % size) for i in range(size)])


def neighbour_rim(edge, offset):
    return from_behind(edge, "tile", offset)


def filter_kernel(rates, blocks):
    cumulative = jnp.cumsum(rates)
    quarter = jnp.sqrt(jnp.sqrt(rates))
    kernel = (
        quarter[:, None]
        * quarter[None, :]
        * jnp.exp(-jnp.abs(cumulative[:, None] - cumulative[None, :]))
    )
    length = rates.shape[0] // blocks
    return kernel.reshape(blocks, length, blocks, length)


def on_device_general(
    forcing,
    transport,
    reactivity,
    jacobian,
    pattern,
    lon_rate,
    lat_rate,
    vertical,
    step_scale,
    control,
):
    adjoint = forcing[0, 0].astype(jnp.float32)
    tile_rows, tile_cols, species = adjoint.shape
    weights = transport[:, 0, 0]
    reacting = reactivity[0, 0][:, :, None]
    groups = pattern.shape[0]
    width = species // groups
    blockmask = jnp.broadcast_to(
        pattern.astype(jnp.float32)[:, None, :, None], (groups, width, groups, width)
    ).reshape(species, species)
    coupling = jacobian[0] * blockmask
    tiles = lax.axis_size("tile")
    lon_tiles = tiles // TJ
    placing = lax.axis_index("tile") % TJ
    keep_south = (placing > 0).astype(jnp.float32)
    keep_north = (placing < TJ - 1).astype(jnp.float32)
    for sweep in range(STEPS):
        if lon_tiles > 1:
            west_rim = neighbour_rim(adjoint[-1], TJ)
            east_rim = neighbour_rim(adjoint[0], -TJ)
        else:
            west_rim = adjoint[-1]
            east_rim = adjoint[0]
        south_rim = neighbour_rim(adjoint[:, -1], 1) * keep_south
        north_rim = neighbour_rim(adjoint[:, 0], -1) * keep_north
        from_west = jnp.concatenate([west_rim[None], adjoint[:-1]], 0)
        from_east = jnp.concatenate([adjoint[1:], east_rim[None]], 0)
        from_south = jnp.concatenate([south_rim[:, None], adjoint[:, :-1]], 1)
        from_north = jnp.concatenate([adjoint[:, 1:], north_rim[:, None]], 1)
        moved = (
            adjoint
            + weights[0][:, :, None] * (from_west - adjoint)
            + weights[1][:, :, None] * (from_east - adjoint)
            + weights[2][:, :, None] * (from_south - adjoint)
            + weights[3][:, :, None] * (from_north - adjoint)
        )
        reacted = jnp.dot(
            moved.reshape(tile_rows * tile_cols, species),
            coupling,
            precision=HIGHEST,
            preferred_element_type=jnp.float32,
        )
        adjoint = moved + reacting * reacted.reshape(tile_rows, tile_cols, species)
    gradient = adjoint.astype(jnp.bfloat16)
    planes = lax.all_to_all(
        gradient.reshape(1, tile_rows * tile_cols, species),
        "tile",
        split_axis=2,
        concat_axis=0,
        tiled=True,
    )
    owned = planes.shape[2]
    planes = jnp.moveaxis(planes.reshape(lon_tiles, TJ, tile_rows, tile_cols, owned), 4, 0)

    def filter_species(inputs):
        lon_line, lat_line, plane = inputs
        lon_kernel = filter_kernel(lon_line, lon_tiles)
        lat_kernel = filter_kernel(lat_line, TJ)
        along_lon = jnp.einsum(
            "abcd,cjdy->ajby", lon_kernel, plane.astype(jnp.float32), precision=HIGHEST
        )
        return jnp.einsum("jykz,akbz->ajby", lat_kernel, along_lon, precision=HIGHEST).astype(
            jnp.bfloat16
        )

    filtered = jnp.moveaxis(lax.map(filter_species, (lon_rate, lat_rate, planes)), 0, 4)
    level_here = lax.axis_index("lev")
    mixing = lax.dynamic_index_in_dim(vertical, level_here, 1, keepdims=False)
    returned = lax.all_to_all(
        filtered.reshape(tiles, tile_rows * tile_cols, owned),
        "tile",
        split_axis=0,
        concat_axis=2,
        tiled=True,
    )
    factor = mixing.T
    summed = jnp.sum(
        lax.all_gather(returned, "lev", axis=0, tiled=True) * factor[:, None, :], axis=0
    )
    increment = summed.reshape(tile_rows, tile_cols, species)
    updated = control[0, 0].astype(jnp.float32) - step_scale * increment
    return updated.astype(jnp.bfloat16)[None, None]


MESH = pl.DeviceIdType.MESH
RIM = STEPS
CHUNK = 10
PIECES = 6


def up_to(size, multiple):
    return -(-size // multiple) * multiple


def fused_kernel(tiles, levels, *refs):
    inputs, out_ref, held, arrived = refs[:10], refs[10], refs[11:21], refs[21]
    (
        forcing_ref,
        transport_ref,
        reactivity_ref,
        jacobian_ref,
        pattern_ref,
        lon_rate_ref,
        lat_rate_ref,
        vertical_ref,
        step_scale_ref,
        control_ref,
    ) = held
    (
        state_a,
        state_b,
        weights_own,
        weights_out,
        weights_rim,
        rim_out,
        rim_in,
        weights,
        moved_ref,
        split_ref,
        plane,
        ahead_ref,
        rates_own,
        rates_all,
        carry_out,
        carry_in,
        fields,
        halo_send,
        halo_recv,
        rim_send,
        rim_recv,
        rate_send,
        rate_recv,
        carry_send,
        carry_recv,
        level_send,
        level_recv,
    ) = refs[22:]
    loads = [
        pltpu.make_async_copy(source, target, arrived.at[k])
        for k, (source, target) in enumerate(zip(inputs, held))
    ]
    for load in loads:
        load.start()
    nlon, nlat, species = forcing_ref.shape
    pitch = state_a.shape[1]
    rows = nlat + 2 * RIM
    rim_rows = rim_out.shape[1]
    owned, lat_total = lat_rate_ref.shape
    lon_at = lat_total
    rate_width = rates_own.shape[1]
    t = lax.axis_index("tile")
    level = lax.axis_index("lev")
    sibling = level + 1 - 2 * lax.rem(level, 2)
    across = lax.rem(level + 2, levels)
    f32, bf16 = jnp.float32, jnp.bfloat16

    barrier = pltpu.get_barrier_semaphore()
    for o in range(1, tiles):
        pl.semaphore_signal(
            barrier, inc=1, device_id=(level, lax.rem(t + o, tiles)), device_id_type=MESH
        )
    for other in (sibling, across):
        pl.semaphore_signal(barrier, inc=1, device_id=(other, t), device_id_type=MESH)

    weights_own[...] = jnp.zeros_like(weights_own)
    rates_own[...] = jnp.zeros_like(rates_own)
    plane[...] = jnp.zeros_like(plane)
    for load in loads[:-1]:
        load.wait()
    weights_own[0:4, 0:nlon, 0:nlat] = transport_ref[...].reshape(4, nlon, nlat)
    weights_own[4, 0:nlon, 0:nlat] = reactivity_ref[...].reshape(nlon, nlat)
    lane = lax.broadcasted_iota(jnp.int32, (pitch, 128), 1)
    thin = RIM - 1
    for side, first in ((0, nlat - thin), (1, 0)):
        packed = jnp.zeros((pitch, 128), f32)
        for d in range(5):
            moved_lanes = pltpu.roll(weights_own[d], (thin * d - first) % 128, 1)
            packed = jnp.where(lane // thin == d, moved_lanes, packed)
        weights_out[side] = packed
    rates_own[:, 0:lat_total] = lat_rate_ref[...]
    rates_own[:, lon_at : lon_at + nlon] = lon_rate_ref[...]
    for i in range(nlon):
        plane[i * pitch : i * pitch + nlat, :] = forcing_ref[i].astype(f32)
    plane[nlon * pitch : nlon * pitch + nlat, :] = forcing_ref[0].astype(f32)
    plane[(pitch - 1) * pitch : (pitch - 1) * pitch + nlat, :] = forcing_ref[nlon - 1].astype(f32)
    for j in range(nlat):
        state_a[RIM + j] = plane[pl.ds(j, pitch, stride=pitch), :]
    for side, first in ((0, nlat), (1, RIM)):
        rim_out[side] = jnp.concatenate(
            [
                state_a[first : first + RIM].reshape(RIM * pitch, species),
                jnp.zeros((rim_rows - RIM * pitch, species), f32),
            ],
            0,
        ).astype(bf16)

    pl.semaphore_wait(barrier, tiles + 1)

    def halo(side):
        place = t + 1 - 2 * side
        return (
            pltpu.make_async_remote_copy(
                src_ref=rim_out.at[side],
                dst_ref=rim_in.at[side],
                send_sem=halo_send.at[side],
                recv_sem=halo_recv.at[side],
                device_id=(level, place),
                device_id_type=MESH,
            ),
            pltpu.make_async_remote_copy(
                src_ref=weights_out.at[side],
                dst_ref=weights_rim.at[side],
                send_sem=rim_send.at[side],
                recv_sem=rim_recv.at[side],
                device_id=(level, place),
                device_id_type=MESH,
            ),
        )

    sends = [halo(0), halo(1)]

    @pl.when(t < tiles - 1)
    def _():
        for copy in sends[0]:
            copy.start()

    @pl.when(t > 0)
    def _():
        for copy in sends[1]:
            copy.start()

    @pl.when(t == 0)
    def _():
        rim_in[0] = jnp.zeros(rim_in.shape[1:], bf16)
        weights_rim[0] = jnp.zeros(weights_rim.shape[1:], f32)

    @pl.when(t == tiles - 1)
    def _():
        rim_in[1] = jnp.zeros(rim_in.shape[1:], bf16)
        weights_rim[1] = jnp.zeros(weights_rim.shape[1:], f32)

    for j in range(nlat):
        weights[:, RIM + j] = jnp.broadcast_to(
            weights_own[:, :, j : j + 1], (5, pitch, species)
        )

    groups = pattern_ref.shape[0]
    width = species // groups
    member = (
        lax.broadcasted_iota(jnp.int32, (species, groups), 0) // width
        == lax.broadcasted_iota(jnp.int32, (species, groups), 1)
    ).astype(f32)
    mask = lax.dot_general(
        jnp.dot(member, pattern_ref[...].astype(f32), preferred_element_type=f32),
        member,
        (((1,), (1,)), ((), ())),
        preferred_element_type=f32,
    )
    coupling = jacobian_ref[...] * mask
    high = coupling.astype(bf16)
    low = (coupling - high.astype(f32)).astype(bf16)
    both = jnp.concatenate(
        [
            jnp.concatenate([high, low], 1),
            jnp.concatenate([high, jnp.zeros_like(low)], 1),
        ],
        0,
    )

    @pl.when(t > 0)
    def _():
        sends[0][0].wait_recv()
        sends[0][1].wait_recv()

    @pl.when(t < tiles - 1)
    def _():
        sends[1][0].wait_recv()
        sends[1][1].wait_recv()

    mine = pl.ds(pl.multiple_of(t * owned, owned), owned)
    rate_copies = []
    for o in range(1, tiles):
        rate_copies.append(
            pltpu.make_async_remote_copy(
                src_ref=rates_own,
                dst_ref=rates_all.at[mine],
                send_sem=rate_send.at[o - 1],
                recv_sem=rate_recv.at[o - 1],
                device_id=(level, lax.rem(t + o, tiles)),
                device_id_type=MESH,
            )
        )
        rate_copies[-1].start()
    rates_all[mine, :] = rates_own[...]

    for side, first in ((0, 0), (1, nlat + RIM)):
        rim = rim_in[side].astype(f32)[: RIM * pitch]
        state_a[first : first + RIM] = rim.reshape(RIM, pitch, species)
        for r in range(thin):
            for d in range(5):
                at = thin * d + r
                weights[d, (1, nlat + RIM)[side] + r] = jnp.broadcast_to(
                    weights_rim[side, :, at : at + 1], (pitch, species)
                )

    @pl.when(t < tiles - 1)
    def _():
        sends[0][0].wait_send()
        sends[0][1].wait_send()

    @pl.when(t > 0)
    def _():
        sends[1][0].wait_send()
        sends[1][1].wait_send()

    def step(source, target, first, last, final):
        for j0 in range(first, last, CHUNK):
            n = min(CHUNK, last - j0)
            for j in range(j0, j0 + n, 2):
                here = source[j : j + 2]
                moved = (
                    here
                    + weights[0, j : j + 2] * (pltpu.roll(here, 1, 1) - here)
                    + weights[1, j : j + 2] * (pltpu.roll(here, pitch - 1, 1) - here)
                    + weights[2, j : j + 2] * (source[j - 1 : j + 1] - here)
                    + weights[3, j : j + 2] * (source[j + 1 : j + 3] - here)
                )
                moved = moved.reshape(2 * pitch, species)
                at = pl.ds((j - first) * pitch, 2 * pitch)
                moved_ref[at, :] = moved
                top = moved.astype(bf16)
                split_ref[at, 0:species] = top
                split_ref[at, species:] = (moved - top.astype(f32)).astype(bf16)
            at = pl.ds((j0 - first) * pitch, n * pitch)
            product = jnp.dot(split_ref[at, :], both, preferred_element_type=f32)
            reacted = product[:, :species] + product[:, species:]
            after = moved_ref[at, :].reshape(n, pitch, species) + weights[
                4, j0 : j0 + n
            ] * reacted.reshape(n, pitch, species)
            if final:
                target[j0 : j0 + n] = after.astype(bf16).astype(f32)
            else:
                target[j0 : j0 + n] = after
                target[j0 : j0 + n, nlon : nlon + 1] = after[:, 0:1]
                target[j0 : j0 + n, pitch - 1 : pitch] = after[:, nlon - 1 : nlon]

    states = [state_a, state_b]
    for sweep in range(STEPS):
        step(
            states[sweep % 2],
            states[(sweep + 1) % 2],
            1 + sweep,
            rows - 1 - sweep,
            sweep == STEPS - 1,
        )
    gradient = states[STEPS % 2]

    for copy in rate_copies:
        copy.wait()
    cell = lax.broadcasted_iota(jnp.int32, (pitch, rate_width), 1)
    row = lax.broadcasted_iota(jnp.int32, (pitch, rate_width), 0)
    start = t * nlat
    lat_cell = cell < lat_total
    picks = jnp.concatenate(
        [
            (cell == start + row) & (row < nlat),
            (cell >= start) & (cell <= start + row) & (cell < start + nlat),
            (cell < row * nlat) & lat_cell,
            (cell == lon_at + row) & (row < nlon),
        ],
        0,
    ).astype(f32)
    lines = lax.dot_general(
        picks,
        rates_all[...],
        (((1,), (1,)), ((), ())),
        precision=HIGHEST,
        preferred_element_type=f32,
    )
    lat_line = lines[0:pitch]
    lat_sum = lines[pitch : 2 * pitch]
    before = lines[2 * pitch : 3 * pitch]
    lon_line = lines[3 * pitch :]
    lat_q, lat_d = jnp.sqrt(jnp.sqrt(lat_line)), jnp.exp(-lat_line)
    lon_q, lon_d = jnp.sqrt(jnp.sqrt(lon_line)), jnp.exp(-lon_line)
    from_south = lat_q * jnp.exp(-lat_sum)
    from_north = lat_q * jnp.exp(lat_sum - lat_sum[nlat - 1 : nlat])

    carry = jnp.zeros((pitch, species), f32)
    for j in range(nlat):
        carry = lat_q[j : j + 1] * gradient[RIM + j] + lat_d[j : j + 1] * carry
        ahead_ref[j] = carry
    carry_out[0] = carry
    carry = jnp.zeros((pitch, species), f32)
    for j in range(nlat - 1, -1, -1):
        item = lat_q[j : j + 1] * gradient[RIM + j]
        later = lat_d[j + 1 : j + 2] * carry if j < nlat - 1 else carry
        carry = item + later
        plane[j * pitch : (j + 1) * pitch, :] = lat_q[j : j + 1] * (ahead_ref[j] + later)
    carry_out[1] = lat_d[0:1] * carry

    carry_copies = []
    for o in range(1, tiles):
        carry_copies.append(
            pltpu.make_async_remote_copy(
                src_ref=carry_out.at[(t + o) // tiles],
                dst_ref=carry_in.at[o - 1],
                send_sem=carry_send.at[o - 1],
                recv_sem=carry_recv.at[o - 1],
                device_id=(level, lax.rem(t + o, tiles)),
                device_id_type=MESH,
            )
        )
        carry_copies[-1].start()

    order = lax.broadcasted_iota(jnp.int32, (pitch, species), 0)

    def before_tile(u):
        return jnp.sum(jnp.where(order == u, before, 0.0), 0, keepdims=True)

    south = jnp.zeros((pitch, species), f32)
    north = jnp.zeros((pitch, species), f32)
    for o in range(1, tiles):
        u = lax.rem(t + tiles - o, tiles)
        upper, lower = jnp.maximum(u, t), jnp.minimum(u, t)
        factor = jnp.exp(before_tile(lower + 1) - before_tile(upper))
        carry_copies[o - 1].wait()
        term = factor * carry_in[o - 1]
        south = south + jnp.where(o <= t, term, 0.0)
        north = north + jnp.where(o <= t, 0.0, term)
    for j in range(nlat):
        at = pl.ds(j * pitch, pitch)
        plane[at, :] = (
            plane[at, :] + from_south[j : j + 1] * south + from_north[j : j + 1] * north
        )

    carry = jnp.zeros((pitch, species), f32)
    for i in range(nlon):
        item = lon_q[i : i + 1] * plane[pl.ds(i, pitch, stride=pitch), :]
        carry = item + lon_d[i : i + 1] * carry
        ahead_ref[i] = carry

    def level_copy(source, target, k, place):
        return pltpu.make_async_remote_copy(
            src_ref=fields.at[source, k],
            dst_ref=fields.at[target, k],
            send_sem=level_send.at[target, k],
            recv_sem=level_recv.at[target, k],
            device_id=(place, t),
            device_id_type=MESH,
        )

    piece = nlon // PIECES
    carry = jnp.zeros((pitch, species), f32)
    far, near, relay = {}, {}, {}
    order_k = range(PIECES - 1, -1, -1)
    for k in order_k:
        for pair in range(piece // 2 - 1, -1, -1):
            done = []
            for i in (k * piece + 2 * pair + 1, k * piece + 2 * pair):
                item = lon_q[i : i + 1] * plane[pl.ds(i, pitch, stride=pitch), :]
                later = lon_d[i + 1 : i + 2] * carry if i < nlon - 1 else carry
                carry = item + later
                done.append(lon_q[i : i + 1] * (ahead_ref[i] + later))
            fields[0, k, 2 * pair * pitch : 2 * (pair + 1) * pitch, :] = jnp.concatenate(
                done[::-1], 0
            ).astype(bf16)
        far[k] = level_copy(0, 2, k, across)
        near[k] = level_copy(0, 1, k, sibling)
        far[k].start()
        near[k].start()

    loads[-1].wait()
    factors = [
        vertical_ref[level, pl.ds(source, 1), :]
        for source in (level, sibling, across, lax.rem(sibling + 2, levels))
    ]
    scale = step_scale_ref[...]

    def finish(k):
        total = factors[0] * fields[0, k].astype(f32)
        for slot in range(1, levels):
            total = total + factors[slot] * fields[slot, k].astype(f32)
        total = (scale * total).reshape(piece, pitch, species)[:, :nlat]
        at = pl.ds(k * piece, piece)
        out_ref[at] = (control_ref[at].astype(f32) - total).astype(bf16)

    previous = None
    for k in order_k:
        far[k].wait_recv()
        relay[k] = level_copy(2, 3, k, sibling)
        relay[k].start()
        near[k].wait_recv()
        if previous is not None:
            relay[previous].wait_recv()
            finish(previous)
        previous = k
    relay[previous].wait_recv()
    finish(previous)
    for k in order_k:
        far[k].wait_send()
        near[k].wait_send()
        relay[k].wait_send()


def on_device_fused(
    tiles,
    levels,
    forcing,
    transport,
    reactivity,
    jacobian,
    pattern,
    lon_rate,
    lat_rate,
    vertical,
    step_scale,
    control,
):
    nlon, nlat, species = forcing.shape[2:]
    pitch = up_to(max(nlon + 2, nlat), 8)
    rows = nlat + 2 * RIM
    owned, lat_total = lat_rate.shape
    rate_width = up_to(lat_total + nlon, 128)
    f32, bf16 = jnp.float32, jnp.bfloat16
    dma = pltpu.SemaphoreType.DMA
    piece_rows = nlon // PIECES * pitch
    rim_rows = up_to(RIM * pitch, 16)
    inputs = (
        forcing[0, 0],
        transport[:, 0, 0][:, :, None],
        reactivity[0, 0][:, None],
        jacobian[0],
        pattern,
        lon_rate,
        lat_rate,
        jnp.transpose(vertical, (1, 2, 0)),
        step_scale[None],
        control[0, 0],
    )
    updated = pl.pallas_call(
        functools.partial(fused_kernel, tiles, levels),
        out_shape=jax.ShapeDtypeStruct((nlon, nlat, species), bf16),
        in_specs=[pl.BlockSpec(memory_space=pltpu.HBM)] * 10,
        out_specs=pl.BlockSpec(memory_space=pltpu.VMEM),
        scratch_shapes=[pltpu.VMEM(x.shape, x.dtype) for x in inputs]
        + [
            dma((len(inputs),)),
            pltpu.VMEM((rows, pitch, species), f32),
            pltpu.VMEM((rows, pitch, species), f32),
            pltpu.VMEM((5, pitch, 128), f32),
            pltpu.VMEM((2, pitch, 128), f32),
            pltpu.VMEM((2, pitch, 128), f32),
            pltpu.VMEM((2, rim_rows, species), bf16),
            pltpu.VMEM((2, rim_rows, species), bf16),
            pltpu.VMEM((5, rows, pitch, species), f32),
            pltpu.VMEM((rows * pitch, species), f32),
            pltpu.VMEM((rows * pitch, 2 * species), bf16),
            pltpu.VMEM((pitch * pitch, species), f32),
            pltpu.VMEM((pitch, pitch, species), f32),
            pltpu.VMEM((owned, rate_width), f32),
            pltpu.VMEM((species, rate_width), f32),
            pltpu.VMEM((2, pitch, species), f32),
            pltpu.VMEM((tiles - 1, pitch, species), f32),
            pltpu.VMEM((levels, PIECES, piece_rows, species), bf16),
            dma((2,)),
            dma((2,)),
            dma((2,)),
            dma((2,)),
            dma((tiles - 1,)),
            dma((tiles - 1,)),
            dma((tiles - 1,)),
            dma((tiles - 1,)),
            dma((levels, PIECES)),
            dma((levels, PIECES)),
        ],
        compiler_params=pltpu.CompilerParams(
            collective_id=0, has_side_effects=True, vmem_limit_bytes=56 * 1024 * 1024
        ),
        name="fused",
    )(*inputs)
    return updated[None, None]


def on_device(forcing, *others):
    tiles, levels = lax.axis_size("tile"), lax.axis_size("lev")
    nlon, nlat, species = forcing.shape[2:]
    one_ring = tiles == TJ and levels == 4
    fits = nlon % (2 * PIECES) == 0 and nlon == nlat and nlat % 2 == 0
    if one_ring and fits and species == 128:
        return on_device_fused(tiles, levels, forcing, *others)
    return on_device_general(forcing, *others)


def solution(mesh):
    in_specs = (
        P("lev", "tile", None, None, None),
        P(None, "lev", "tile", None, None),
        P("lev", "tile", None, None),
        P("lev", None, None),
        P(),
        P("tile", None),
        P("tile", None),
        P(),
        P(),
        P("lev", "tile", None, None, None),
    )
    out_specs = P("lev", "tile", None, None, None)
    return jax.shard_map(
        on_device, mesh=mesh, in_specs=in_specs, out_specs=out_specs, check_vma=False
    )
```

```python
import functools

import jax
import jax.numpy as jnp
from jax import lax
from jax.experimental import pallas as pl
from jax.experimental.pallas import tpu as pltpu
from jax.sharding import PartitionSpec as P

TJ = 8
STEPS = 3


HIGHEST = lax.Precision.HIGHEST


def from_behind(x, axis, by):
    size = lax.axis_size(axis)
    return lax.ppermute(x, axis, [(i, (i + by) % size) for i in range(size)])


def neighbour_rim(edge, offset):
    return from_behind(edge, "tile", offset)


def filter_kernel(rates, blocks):
    cumulative = jnp.cumsum(rates)
    quarter = jnp.sqrt(jnp.sqrt(rates))
    kernel = (
        quarter[:, None]
        * quarter[None, :]
        * jnp.exp(-jnp.abs(cumulative[:, None] - cumulative[None, :]))
    )
    length = rates.shape[0] // blocks
    return kernel.reshape(blocks, length, blocks, length)


def on_device_general(
    forcing,
    transport,
    reactivity,
    jacobian,
    pattern,
    lon_rate,
    lat_rate,
    vertical,
    step_scale,
    control,
):
    adjoint = forcing[0, 0].astype(jnp.float32)
    tile_rows, tile_cols, species = adjoint.shape
    weights = transport[:, 0, 0]
    reacting = reactivity[0, 0][:, :, None]
    groups = pattern.shape[0]
    width = species // groups
    blockmask = jnp.broadcast_to(
        pattern.astype(jnp.float32)[:, None, :, None], (groups, width, groups, width)
    ).reshape(species, species)
    coupling = jacobian[0] * blockmask
    tiles = lax.axis_size("tile")
    lon_tiles = tiles // TJ
    placing = lax.axis_index("tile") % TJ
    keep_south = (placing > 0).astype(jnp.float32)
    keep_north = (placing < TJ - 1).astype(jnp.float32)
    for sweep in range(STEPS):
        if lon_tiles > 1:
            west_rim = neighbour_rim(adjoint[-1], TJ)
            east_rim = neighbour_rim(adjoint[0], -TJ)
        else:
            west_rim = adjoint[-1]
            east_rim = adjoint[0]
        south_rim = neighbour_rim(adjoint[:, -1], 1) * keep_south
        north_rim = neighbour_rim(adjoint[:, 0], -1) * keep_north
        from_west = jnp.concatenate([west_rim[None], adjoint[:-1]], 0)
        from_east = jnp.concatenate([adjoint[1:], east_rim[None]], 0)
        from_south = jnp.concatenate([south_rim[:, None], adjoint[:, :-1]], 1)
        from_north = jnp.concatenate([adjoint[:, 1:], north_rim[:, None]], 1)
        moved = (
            adjoint
            + weights[0][:, :, None] * (from_west - adjoint)
            + weights[1][:, :, None] * (from_east - adjoint)
            + weights[2][:, :, None] * (from_south - adjoint)
            + weights[3][:, :, None] * (from_north - adjoint)
        )
        reacted = jnp.dot(
            moved.reshape(tile_rows * tile_cols, species),
            coupling,
            precision=HIGHEST,
            preferred_element_type=jnp.float32,
        )
        adjoint = moved + reacting * reacted.reshape(tile_rows, tile_cols, species)
    gradient = adjoint.astype(jnp.bfloat16)
    planes = lax.all_to_all(
        gradient.reshape(1, tile_rows * tile_cols, species),
        "tile",
        split_axis=2,
        concat_axis=0,
        tiled=True,
    )
    owned = planes.shape[2]
    planes = jnp.moveaxis(planes.reshape(lon_tiles, TJ, tile_rows, tile_cols, owned), 4, 0)

    def filter_species(inputs):
        lon_line, lat_line, plane = inputs
        lon_kernel = filter_kernel(lon_line, lon_tiles)
        lat_kernel = filter_kernel(lat_line, TJ)
        along_lon = jnp.einsum(
            "abcd,cjdy->ajby", lon_kernel, plane.astype(jnp.float32), precision=HIGHEST
        )
        return jnp.einsum("jykz,akbz->ajby", lat_kernel, along_lon, precision=HIGHEST).astype(
            jnp.bfloat16
        )

    filtered = jnp.moveaxis(lax.map(filter_species, (lon_rate, lat_rate, planes)), 0, 4)
    level_here = lax.axis_index("lev")
    mixing = lax.dynamic_index_in_dim(vertical, level_here, 1, keepdims=False)
    returned = lax.all_to_all(
        filtered.reshape(tiles, tile_rows * tile_cols, owned),
        "tile",
        split_axis=0,
        concat_axis=2,
        tiled=True,
    )
    factor = mixing.T
    summed = jnp.sum(
        lax.all_gather(returned, "lev", axis=0, tiled=True) * factor[:, None, :], axis=0
    )
    increment = summed.reshape(tile_rows, tile_cols, species)
    updated = control[0, 0].astype(jnp.float32) - step_scale * increment
    return updated.astype(jnp.bfloat16)[None, None]


MESH = pl.DeviceIdType.MESH
RIM = STEPS
CHUNK = 10
GROUP = 8


def up_to(size, multiple):
    return -(-size // multiple) * multiple


def fused_kernel(tiles, levels, *refs):
    inputs, out_ref, held, arrived = refs[:10], refs[10], refs[11:21], refs[21]
    (
        forcing_ref,
        transport_ref,
        reactivity_ref,
        jacobian_ref,
        pattern_ref,
        lon_rate_ref,
        lat_rate_ref,
        vertical_ref,
        step_scale_ref,
        control_ref,
    ) = held
    (
        state_a,
        state_b,
        weights_own,
        weights_out,
        weights_rim,
        rim_out,
        rim_in,
        weights,
        moved_ref,
        split_ref,
        plane,
        ahead_ref,
        rates_own,
        rates_all,
        carry_out,
        carry_in,
        plane_far,
        lines_own,
        lines_far,
        grad_out,
        grad_in,
        fields,
        halo_send,
        halo_recv,
        rim_send,
        rim_recv,
        rate_send,
        rate_recv,
        carry_send,
        carry_recv,
        grad_send,
        grad_recv,
        both_send,
        both_recv,
        level_send,
        level_recv,
    ) = refs[22:]
    loads = [
        pltpu.make_async_copy(source, target, arrived.at[k])
        for k, (source, target) in enumerate(zip(inputs, held))
    ]
    for load in loads:
        load.start()
    nlon, nlat, species = forcing_ref.shape
    pitch = state_a.shape[1]
    rows = nlat + 2 * RIM
    rim_rows = rim_out.shape[1]
    owned, lat_total = lat_rate_ref.shape
    lon_at = lat_total
    rate_width = rates_own.shape[1]
    t = lax.axis_index("tile")
    level = lax.axis_index("lev")
    sibling = level + 1 - 2 * lax.rem(level, 2)
    across = lax.rem(level + 2, levels)
    f32, bf16 = jnp.float32, jnp.bfloat16

    barrier = pltpu.get_barrier_semaphore()
    for o in range(1, tiles):
        pl.semaphore_signal(
            barrier, inc=1, device_id=(level, lax.rem(t + o, tiles)), device_id_type=MESH
        )
    for other in (sibling, across):
        pl.semaphore_signal(barrier, inc=1, device_id=(other, t), device_id_type=MESH)

    weights_own[...] = jnp.zeros_like(weights_own)
    rates_own[...] = jnp.zeros_like(rates_own)
    plane[...] = jnp.zeros_like(plane)
    for load in loads[:-1]:
        load.wait()
    weights_own[0:4, 0:nlon, 0:nlat] = transport_ref[...].reshape(4, nlon, nlat)
    weights_own[4, 0:nlon, 0:nlat] = reactivity_ref[...].reshape(nlon, nlat)
    lane = lax.broadcasted_iota(jnp.int32, (pitch, 128), 1)
    thin = RIM - 1
    for side, first in ((0, nlat - thin), (1, 0)):
        packed = jnp.zeros((pitch, 128), f32)
        for d in range(5):
            moved_lanes = pltpu.roll(weights_own[d], (thin * d - first) % 128, 1)
            packed = jnp.where(lane // thin == d, moved_lanes, packed)
        weights_out[side] = packed
    rates_own[:, 0:lat_total] = lat_rate_ref[...]
    rates_own[:, lon_at : lon_at + nlon] = lon_rate_ref[...]
    for i in range(nlon):
        plane[i * pitch : i * pitch + nlat, :] = forcing_ref[i].astype(f32)
    plane[nlon * pitch : nlon * pitch + nlat, :] = forcing_ref[0].astype(f32)
    plane[(pitch - 1) * pitch : (pitch - 1) * pitch + nlat, :] = forcing_ref[nlon - 1].astype(f32)
    for j in range(nlat):
        state_a[RIM + j] = plane[pl.ds(j, pitch, stride=pitch), :]
    for side, first in ((0, nlat), (1, RIM)):
        rim_out[side] = jnp.concatenate(
            [
                state_a[first : first + RIM].reshape(RIM * pitch, species),
                jnp.zeros((rim_rows - RIM * pitch, species), f32),
            ],
            0,
        ).astype(bf16)

    pl.semaphore_wait(barrier, tiles + 1)

    def halo(side):
        place = t + 1 - 2 * side
        return (
            pltpu.make_async_remote_copy(
                src_ref=rim_out.at[side],
                dst_ref=rim_in.at[side],
                send_sem=halo_send.at[side],
                recv_sem=halo_recv.at[side],
                device_id=(level, place),
                device_id_type=MESH,
            ),
            pltpu.make_async_remote_copy(
                src_ref=weights_out.at[side],
                dst_ref=weights_rim.at[side],
                send_sem=rim_send.at[side],
                recv_sem=rim_recv.at[side],
                device_id=(level, place),
                device_id_type=MESH,
            ),
        )

    sends = [halo(0), halo(1)]

    @pl.when(t < tiles - 1)
    def _():
        for copy in sends[0]:
            copy.start()

    @pl.when(t > 0)
    def _():
        for copy in sends[1]:
            copy.start()

    @pl.when(t == 0)
    def _():
        rim_in[0] = jnp.zeros(rim_in.shape[1:], bf16)
        weights_rim[0] = jnp.zeros(weights_rim.shape[1:], f32)

    @pl.when(t == tiles - 1)
    def _():
        rim_in[1] = jnp.zeros(rim_in.shape[1:], bf16)
        weights_rim[1] = jnp.zeros(weights_rim.shape[1:], f32)

    for j in range(nlat):
        weights[:, RIM + j] = jnp.broadcast_to(
            weights_own[:, :, j : j + 1], (5, pitch, species)
        )

    groups = pattern_ref.shape[0]
    width = species // groups
    member = (
        lax.broadcasted_iota(jnp.int32, (species, groups), 0) // width
        == lax.broadcasted_iota(jnp.int32, (species, groups), 1)
    ).astype(f32)
    mask = lax.dot_general(
        jnp.dot(member, pattern_ref[...].astype(f32), preferred_element_type=f32),
        member,
        (((1,), (1,)), ((), ())),
        preferred_element_type=f32,
    )
    coupling = jacobian_ref[...] * mask
    high = coupling.astype(bf16)
    low = (coupling - high.astype(f32)).astype(bf16)
    both = jnp.concatenate(
        [
            jnp.concatenate([high, low], 1),
            jnp.concatenate([high, jnp.zeros_like(low)], 1),
        ],
        0,
    )

    @pl.when(t > 0)
    def _():
        sends[0][0].wait_recv()
        sends[0][1].wait_recv()

    @pl.when(t < tiles - 1)
    def _():
        sends[1][0].wait_recv()
        sends[1][1].wait_recv()

    mine = pl.ds(pl.multiple_of(t * owned, owned), owned)
    rate_copies = []
    for o in range(1, tiles):
        rate_copies.append(
            pltpu.make_async_remote_copy(
                src_ref=rates_own,
                dst_ref=rates_all.at[mine],
                send_sem=rate_send.at[o - 1],
                recv_sem=rate_recv.at[o - 1],
                device_id=(level, lax.rem(t + o, tiles)),
                device_id_type=MESH,
            )
        )
        rate_copies[-1].start()
    rates_all[mine, :] = rates_own[...]

    for side, first in ((0, 0), (1, nlat + RIM)):
        rim = rim_in[side].astype(f32)[: RIM * pitch]
        state_a[first : first + RIM] = rim.reshape(RIM, pitch, species)
        for r in range(thin):
            for d in range(5):
                at = thin * d + r
                weights[d, (1, nlat + RIM)[side] + r] = jnp.broadcast_to(
                    weights_rim[side, :, at : at + 1], (pitch, species)
                )

    @pl.when(t < tiles - 1)
    def _():
        sends[0][0].wait_send()
        sends[0][1].wait_send()

    @pl.when(t > 0)
    def _():
        sends[1][0].wait_send()
        sends[1][1].wait_send()

    def step(source, target, first, last, final):
        chunk = GROUP if final else CHUNK
        for j0 in range(first, last, chunk):
            n = min(chunk, last - j0)
            for j in range(j0, j0 + n, 2):
                here = source[j : j + 2]
                moved = (
                    here
                    + weights[0, j : j + 2] * (pltpu.roll(here, 1, 1) - here)
                    + weights[1, j : j + 2] * (pltpu.roll(here, pitch - 1, 1) - here)
                    + weights[2, j : j + 2] * (source[j - 1 : j + 1] - here)
                    + weights[3, j : j + 2] * (source[j + 1 : j + 3] - here)
                )
                moved = moved.reshape(2 * pitch, species)
                at = pl.ds((j - first) * pitch, 2 * pitch)
                moved_ref[at, :] = moved
                top = moved.astype(bf16)
                split_ref[at, 0:species] = top
                split_ref[at, species:] = (moved - top.astype(f32)).astype(bf16)
            at = pl.ds((j0 - first) * pitch, n * pitch)
            product = jnp.dot(split_ref[at, :], both, preferred_element_type=f32)
            reacted = product[:, :species] + product[:, species:]
            after = moved_ref[at, :].reshape(n, pitch, species) + weights[
                4, j0 : j0 + n
            ] * reacted.reshape(n, pitch, species)
            if final:
                rounded = after.reshape(n * pitch, species).astype(bf16)
                plane[at, :] = rounded.astype(f32)
                grad_out[at, :] = rounded
                grad_copies[(j0 - first) // GROUP].start()
            else:
                target[j0 : j0 + n] = after
                target[j0 : j0 + n, nlon : nlon + 1] = after[:, 0:1]
                target[j0 : j0 + n, pitch - 1 : pitch] = after[:, nlon - 1 : nlon]

    groups_at = [(k, min(GROUP, nlat - k)) for k in range(0, nlat, GROUP)]

    def rows_of(k):
        return pl.ds(groups_at[k][0] * pitch, groups_at[k][1] * pitch)

    grad_copies = [
        pltpu.make_async_remote_copy(
            src_ref=grad_out.at[rows_of(k)],
            dst_ref=grad_in.at[rows_of(k)],
            send_sem=grad_send.at[k],
            recv_sem=grad_recv.at[k],
            device_id=(across, t),
            device_id_type=MESH,
        )
        for k in range(len(groups_at))
    ]
    spare = pl.ds((nlat + 2) * pitch, (pitch - nlat - 2) * pitch)
    for buffer in (plane, plane_far):
        buffer[spare, :] = jnp.zeros(((pitch - nlat - 2) * pitch, species), f32)
    spare = pl.ds(nlon * pitch, (pitch - nlon) * pitch)
    for buffer in (lines_own, lines_far):
        buffer[spare, :] = jnp.zeros(((pitch - nlon) * pitch, species), f32)

    states = [state_a, state_b]
    for sweep in range(STEPS):
        step(
            states[sweep % 2],
            states[(sweep + 1) % 2],
            1 + sweep,
            rows - 1 - sweep,
            sweep == STEPS - 1,
        )
    for copy in rate_copies:
        copy.wait()
    cell = lax.broadcasted_iota(jnp.int32, (pitch, rate_width), 1)
    row = lax.broadcasted_iota(jnp.int32, (pitch, rate_width), 0)
    start = t * nlat
    lat_cell = cell < lat_total
    picks = jnp.concatenate(
        [
            (cell == start + row) & (row < nlat),
            (cell < row * nlat) & lat_cell,
            (cell == lon_at + row) & (row < nlon),
        ],
        0,
    ).astype(f32)
    lines = lax.dot_general(
        picks,
        rates_all[...],
        (((1,), (1,)), ((), ())),
        precision=HIGHEST,
        preferred_element_type=f32,
    )
    lat_line = lines[0:pitch]
    before = lines[pitch : 2 * pitch]
    lon_line = lines[2 * pitch :]
    lat_q, lat_d = jnp.sqrt(jnp.sqrt(lat_line)), jnp.exp(-lat_line)
    lon_q, lon_d = jnp.sqrt(jnp.sqrt(lon_line)), jnp.exp(-lon_line)

    carry = jnp.zeros((pitch, species), f32)
    for j in range(nlat):
        at = pl.ds(j * pitch, pitch)
        carry = lat_q[j : j + 1] * plane[at, :] + lat_d[j : j + 1] * carry
    carry_out[0] = carry
    carry = jnp.zeros((pitch, species), f32)
    for j in range(nlat - 1, -1, -1):
        at = pl.ds(j * pitch, pitch)
        carry = lat_d[j : j + 1] * (lat_q[j : j + 1] * plane[at, :] + carry)
    carry_out[1] = carry

    carry_copies = []
    for o in range(1, tiles):
        carry_copies.append(
            pltpu.make_async_remote_copy(
                src_ref=carry_out.at[(t + o) // tiles],
                dst_ref=carry_in.at[o - 1],
                send_sem=carry_send.at[o - 1],
                recv_sem=carry_recv.at[o - 1],
                device_id=(level, lax.rem(t + o, tiles)),
                device_id_type=MESH,
            )
        )
        carry_copies[-1].start()

    def along_lon(source, target, first, n):
        def item(i):
            cells = source[pl.ds(first * pitch + i, n, stride=pitch), :]
            return lon_q[i : i + 1] * cells

        carry = jnp.zeros((n, species), f32)
        for i in range(nlon):
            carry = item(i) + lon_d[i : i + 1] * carry
            target[pl.ds(i * pitch + first, n), :] = carry
        later = jnp.zeros((n, species), f32)
        for i in range(nlon - 1, -1, -1):
            at = pl.ds(i * pitch + first, n)
            target[at, :] = lon_q[i : i + 1] * (target[at, :] + later)
            later = lon_d[i : i + 1] * (item(i) + later)

    def take(k):
        grad_copies[k].wait_recv()
        plane_far[rows_of(k), :] = grad_in[rows_of(k), :].astype(f32)

    split_at = len(groups_at) // 2
    along_lon(plane, lines_own, 0, (len(groups_at) - 1) * GROUP)
    for k in range(split_at):
        take(k)
        along_lon(plane_far, lines_far, k * GROUP, GROUP)

    order = lax.broadcasted_iota(jnp.int32, (pitch, species), 0)

    def before_tile(u):
        return jnp.sum(jnp.where(order == u, before, 0.0), 0, keepdims=True)

    south = jnp.zeros((pitch, species), f32)
    north = jnp.zeros((pitch, species), f32)
    for o in range(1, tiles):
        u = lax.rem(t + tiles - o, tiles)
        upper, lower = jnp.maximum(u, t), jnp.minimum(u, t)
        factor = jnp.exp(before_tile(lower + 1) - before_tile(upper))
        carry_copies[o - 1].wait()
        term = factor * carry_in[o - 1]
        south = south + jnp.where(o <= t, term, 0.0)
        north = north + jnp.where(o <= t, 0.0, term)
    plane[nlat * pitch : (nlat + 1) * pitch, :] = south
    plane[(nlat + 1) * pitch : (nlat + 2) * pitch, :] = north
    carried = pl.ds(nlat * pitch, 2 * pitch)
    both_copy = pltpu.make_async_remote_copy(
        src_ref=plane.at[carried],
        dst_ref=plane_far.at[carried],
        send_sem=both_send,
        recv_sem=both_recv,
        device_id=(across, t),
        device_id_type=MESH,
    )
    both_copy.start()

    def along_lat(lines_ref, slot):
        def line(j):
            return lines_ref[pl.ds(j, pitch, stride=pitch), :]

        carry = line(nlat)
        for j in range(nlat):
            carry = lat_q[j : j + 1] * line(j) + lat_d[j : j + 1] * carry
            ahead_ref[j] = carry
        later = line(nlat + 1)
        copies = {}
        for k in range(len(groups_at) - 1, -1, -1):
            first, n = groups_at[k]
            for j in range(first + n - 2, first - 1, -2):
                done = []
                for row_at in (j + 1, j):
                    q = lat_q[row_at : row_at + 1]
                    done.append(q * (ahead_ref[row_at] + later))
                    later = lat_d[row_at : row_at + 1] * (q * line(row_at) + later)
                fields[slot, pl.ds(j * pitch, 2 * pitch), :] = jnp.concatenate(
                    done[::-1], 0
                ).astype(bf16)
            copies[k] = pltpu.make_async_remote_copy(
                src_ref=fields.at[slot, rows_of(k)],
                dst_ref=fields.at[slot + 1, rows_of(k)],
                send_sem=level_send.at[slot // 2, k],
                recv_sem=level_recv.at[slot // 2, k],
                device_id=(sibling, t),
                device_id_type=MESH,
            )
            copies[k].start()
        return copies

    last_group = len(groups_at) - 1
    along_lon(plane, lines_own, last_group * GROUP, pitch - last_group * GROUP)
    near = along_lat(lines_own, 0)
    for k in range(split_at, len(groups_at)):
        take(k)
        if k < last_group:
            along_lon(plane_far, lines_far, k * GROUP, GROUP)
    both_copy.wait_recv()
    along_lon(plane_far, lines_far, last_group * GROUP, pitch - last_group * GROUP)
    relay = along_lat(lines_far, 2)

    loads[-1].wait()
    factors = [
        vertical_ref[level, pl.ds(source, 1), :]
        for source in (level, sibling, across, lax.rem(sibling + 2, levels))
    ]
    scale = step_scale_ref[...]
    for k in range(last_group, -1, -1):
        near[k].wait_recv()
        relay[k].wait_recv()
        at = rows_of(k)
        total = factors[0] * fields[0, at, :].astype(f32)
        for slot in range(1, levels):
            total = total + factors[slot] * fields[slot, at, :].astype(f32)
        moved_ref[at, :] = scale * total
    for i in range(nlon):
        total = moved_ref[pl.ds(i, pitch, stride=pitch), :]
        out_ref[i] = (control_ref[i].astype(f32) - total[:nlat]).astype(bf16)
    both_copy.wait_send()
    for k in range(len(groups_at)):
        grad_copies[k].wait_send()
        near[k].wait_send()
        relay[k].wait_send()


def on_device_fused(
    tiles,
    levels,
    forcing,
    transport,
    reactivity,
    jacobian,
    pattern,
    lon_rate,
    lat_rate,
    vertical,
    step_scale,
    control,
):
    nlon, nlat, species = forcing.shape[2:]
    pitch = up_to(max(nlon + 2, nlat), 8)
    rows = nlat + 2 * RIM
    owned, lat_total = lat_rate.shape
    rate_width = up_to(lat_total + nlon, 128)
    f32, bf16 = jnp.float32, jnp.bfloat16
    dma = pltpu.SemaphoreType.DMA
    count = -(-nlat // GROUP)
    rim_rows = up_to(RIM * pitch, 16)
    inputs = (
        forcing[0, 0],
        transport[:, 0, 0][:, :, None],
        reactivity[0, 0][:, None],
        jacobian[0],
        pattern,
        lon_rate,
        lat_rate,
        jnp.transpose(vertical, (1, 2, 0)),
        step_scale[None],
        control[0, 0],
    )
    updated = pl.pallas_call(
        functools.partial(fused_kernel, tiles, levels),
        out_shape=jax.ShapeDtypeStruct((nlon, nlat, species), bf16),
        in_specs=[pl.BlockSpec(memory_space=pltpu.HBM)] * 10,
        out_specs=pl.BlockSpec(memory_space=pltpu.VMEM),
        scratch_shapes=[pltpu.VMEM(x.shape, x.dtype) for x in inputs]
        + [
            dma((len(inputs),)),
            pltpu.VMEM((rows, pitch, species), f32),
            pltpu.VMEM((rows, pitch, species), f32),
            pltpu.VMEM((5, pitch, 128), f32),
            pltpu.VMEM((2, pitch, 128), f32),
            pltpu.VMEM((2, pitch, 128), f32),
            pltpu.VMEM((2, rim_rows, species), bf16),
            pltpu.VMEM((2, rim_rows, species), bf16),
            pltpu.VMEM((5, rows, pitch, species), f32),
            pltpu.VMEM((rows * pitch, species), f32),
            pltpu.VMEM((rows * pitch, 2 * species), bf16),
            pltpu.VMEM((pitch * pitch, species), f32),
            pltpu.VMEM((pitch, pitch, species), f32),
            pltpu.VMEM((owned, rate_width), f32),
            pltpu.VMEM((species, rate_width), f32),
            pltpu.VMEM((2, pitch, species), f32),
            pltpu.VMEM((tiles - 1, pitch, species), f32),
            pltpu.VMEM((pitch * pitch, species), f32),
            pltpu.VMEM((pitch * pitch, species), f32),
            pltpu.VMEM((pitch * pitch, species), f32),
            pltpu.VMEM((nlat * pitch, species), bf16),
            pltpu.VMEM((nlat * pitch, species), bf16),
            pltpu.VMEM((levels, nlat * pitch, species), bf16),
            dma((2,)),
            dma((2,)),
            dma((2,)),
            dma((2,)),
            dma((tiles - 1,)),
            dma((tiles - 1,)),
            dma((tiles - 1,)),
            dma((tiles - 1,)),
            dma((count,)),
            dma((count,)),
            dma,
            dma,
            dma((2, count)),
            dma((2, count)),
        ],
        compiler_params=pltpu.CompilerParams(
            collective_id=0, has_side_effects=True, vmem_limit_bytes=56 * 1024 * 1024
        ),
        name="fused",
    )(*inputs)
    return updated[None, None]


def on_device(forcing, *others):
    tiles, levels = lax.axis_size("tile"), lax.axis_size("lev")
    nlon, nlat, species = forcing.shape[2:]
    one_ring = tiles == TJ and levels == 4
    fits = nlon == nlat and nlat % GROUP in (2, 4) and nlat + 2 * RIM <= 128
    if one_ring and fits and species == 128:
        return on_device_fused(tiles, levels, forcing, *others)
    return on_device_general(forcing, *others)


def solution(mesh):
    in_specs = (
        P("lev", "tile", None, None, None),
        P(None, "lev", "tile", None, None),
        P("lev", "tile", None, None),
        P("lev", None, None),
        P(),
        P("tile", None),
        P("tile", None),
        P(),
        P(),
        P("lev", "tile", None, None, None),
    )
    out_specs = P("lev", "tile", None, None, None)
    return jax.shard_map(
        on_device, mesh=mesh, in_specs=in_specs, out_specs=out_specs, check_vma=False
    )
```

```python
import functools

import jax
import jax.numpy as jnp
from jax import lax
from jax.experimental import pallas as pl
from jax.experimental.pallas import tpu as pltpu
from jax.sharding import PartitionSpec as P

TJ = 8
STEPS = 3


HIGHEST = lax.Precision.HIGHEST


def from_behind(x, axis, by):
    size = lax.axis_size(axis)
    return lax.ppermute(x, axis, [(i, (i + by) % size) for i in range(size)])


def neighbour_rim(edge, offset):
    return from_behind(edge, "tile", offset)


def filter_kernel(rates, blocks):
    cumulative = jnp.cumsum(rates)
    quarter = jnp.sqrt(jnp.sqrt(rates))
    kernel = (
        quarter[:, None]
        * quarter[None, :]
        * jnp.exp(-jnp.abs(cumulative[:, None] - cumulative[None, :]))
    )
    length = rates.shape[0] // blocks
    return kernel.reshape(blocks, length, blocks, length)


def on_device_general(
    forcing,
    transport,
    reactivity,
    jacobian,
    pattern,
    lon_rate,
    lat_rate,
    vertical,
    step_scale,
    control,
):
    adjoint = forcing[0, 0].astype(jnp.float32)
    tile_rows, tile_cols, species = adjoint.shape
    weights = transport[:, 0, 0]
    reacting = reactivity[0, 0][:, :, None]
    groups = pattern.shape[0]
    width = species // groups
    blockmask = jnp.broadcast_to(
        pattern.astype(jnp.float32)[:, None, :, None], (groups, width, groups, width)
    ).reshape(species, species)
    coupling = jacobian[0] * blockmask
    tiles = lax.axis_size("tile")
    lon_tiles = tiles // TJ
    placing = lax.axis_index("tile") % TJ
    keep_south = (placing > 0).astype(jnp.float32)
    keep_north = (placing < TJ - 1).astype(jnp.float32)
    for sweep in range(STEPS):
        if lon_tiles > 1:
            west_rim = neighbour_rim(adjoint[-1], TJ)
            east_rim = neighbour_rim(adjoint[0], -TJ)
        else:
            west_rim = adjoint[-1]
            east_rim = adjoint[0]
        south_rim = neighbour_rim(adjoint[:, -1], 1) * keep_south
        north_rim = neighbour_rim(adjoint[:, 0], -1) * keep_north
        from_west = jnp.concatenate([west_rim[None], adjoint[:-1]], 0)
        from_east = jnp.concatenate([adjoint[1:], east_rim[None]], 0)
        from_south = jnp.concatenate([south_rim[:, None], adjoint[:, :-1]], 1)
        from_north = jnp.concatenate([adjoint[:, 1:], north_rim[:, None]], 1)
        moved = (
            adjoint
            + weights[0][:, :, None] * (from_west - adjoint)
            + weights[1][:, :, None] * (from_east - adjoint)
            + weights[2][:, :, None] * (from_south - adjoint)
            + weights[3][:, :, None] * (from_north - adjoint)
        )
        reacted = jnp.dot(
            moved.reshape(tile_rows * tile_cols, species),
            coupling,
            precision=HIGHEST,
            preferred_element_type=jnp.float32,
        )
        adjoint = moved + reacting * reacted.reshape(tile_rows, tile_cols, species)
    gradient = adjoint.astype(jnp.bfloat16)
    planes = lax.all_to_all(
        gradient.reshape(1, tile_rows * tile_cols, species),
        "tile",
        split_axis=2,
        concat_axis=0,
        tiled=True,
    )
    owned = planes.shape[2]
    planes = jnp.moveaxis(planes.reshape(lon_tiles, TJ, tile_rows, tile_cols, owned), 4, 0)

    def filter_species(inputs):
        lon_line, lat_line, plane = inputs
        lon_kernel = filter_kernel(lon_line, lon_tiles)
        lat_kernel = filter_kernel(lat_line, TJ)
        along_lon = jnp.einsum(
            "abcd,cjdy->ajby", lon_kernel, plane.astype(jnp.float32), precision=HIGHEST
        )
        return jnp.einsum("jykz,akbz->ajby", lat_kernel, along_lon, precision=HIGHEST).astype(
            jnp.bfloat16
        )

    filtered = jnp.moveaxis(lax.map(filter_species, (lon_rate, lat_rate, planes)), 0, 4)
    level_here = lax.axis_index("lev")
    mixing = lax.dynamic_index_in_dim(vertical, level_here, 1, keepdims=False)
    returned = lax.all_to_all(
        filtered.reshape(tiles, tile_rows * tile_cols, owned),
        "tile",
        split_axis=0,
        concat_axis=2,
        tiled=True,
    )
    factor = mixing.T
    summed = jnp.sum(
        lax.all_gather(returned, "lev", axis=0, tiled=True) * factor[:, None, :], axis=0
    )
    increment = summed.reshape(tile_rows, tile_cols, species)
    updated = control[0, 0].astype(jnp.float32) - step_scale * increment
    return updated.astype(jnp.bfloat16)[None, None]


MESH = pl.DeviceIdType.MESH
RIM = STEPS
CHUNK = 10
GROUP = 8


def up_to(size, multiple):
    return -(-size // multiple) * multiple


def fused_kernel(tiles, levels, *refs):
    inputs, out_ref, held, arrived = refs[:10], refs[10], refs[11:21], refs[21]
    (
        forcing_ref,
        transport_ref,
        reactivity_ref,
        jacobian_ref,
        pattern_ref,
        lon_rate_ref,
        lat_rate_ref,
        vertical_ref,
        step_scale_ref,
        control_ref,
    ) = held
    (
        state_a,
        state_b,
        weights_own,
        weights_out,
        weights_rim,
        rim_out,
        rim_in,
        weights,
        moved_ref,
        split_ref,
        plane,
        ahead_ref,
        rates_own,
        rates_all,
        carry_out,
        carry_in,
        plane_far,
        lines_own,
        lines_far,
        grad_out,
        grad_in,
        fields,
        halo_send,
        halo_recv,
        rim_send,
        rim_recv,
        rate_send,
        rate_recv,
        carry_send,
        carry_recv,
        grad_send,
        grad_recv,
        both_send,
        both_recv,
        level_send,
        level_recv,
    ) = refs[22:]
    loads = [
        pltpu.make_async_copy(source, target, arrived.at[k])
        for k, (source, target) in enumerate(zip(inputs, held))
    ]
    for load in loads:
        load.start()
    nlon, nlat, species = forcing_ref.shape
    pitch = state_a.shape[1]
    rows = nlat + 2 * RIM
    rim_rows = rim_out.shape[1]
    owned, lat_total = lat_rate_ref.shape
    lon_at = lat_total
    rate_width = rates_own.shape[1]
    t = lax.axis_index("tile")
    level = lax.axis_index("lev")
    sibling = level + 1 - 2 * lax.rem(level, 2)
    across = lax.rem(level + 2, levels)
    f32, bf16 = jnp.float32, jnp.bfloat16

    barrier = pltpu.get_barrier_semaphore()
    for o in range(1, tiles):
        pl.semaphore_signal(
            barrier, inc=1, device_id=(level, lax.rem(t + o, tiles)), device_id_type=MESH
        )
    for other in (sibling, across):
        pl.semaphore_signal(barrier, inc=1, device_id=(other, t), device_id_type=MESH)

    weights_own[...] = jnp.zeros_like(weights_own)
    rates_own[...] = jnp.zeros_like(rates_own)
    plane[...] = jnp.zeros_like(plane)
    for load in loads[:-1]:
        load.wait()
    weights_own[0:4, 0:nlon, 0:nlat] = transport_ref[...].reshape(4, nlon, nlat)
    weights_own[4, 0:nlon, 0:nlat] = reactivity_ref[...].reshape(nlon, nlat)
    lane = lax.broadcasted_iota(jnp.int32, (pitch, 128), 1)
    thin = RIM - 1
    for side, first in ((0, nlat - thin), (1, 0)):
        packed = jnp.zeros((pitch, 128), f32)
        for d in range(5):
            moved_lanes = pltpu.roll(weights_own[d], (thin * d - first) % 128, 1)
            packed = jnp.where(lane // thin == d, moved_lanes, packed)
        weights_out[side] = packed
    rates_own[:, 0:lat_total] = lat_rate_ref[...]
    rates_own[:, lon_at : lon_at + nlon] = lon_rate_ref[...]
    for i in range(nlon):
        plane[i * pitch : i * pitch + nlat, :] = forcing_ref[i].astype(f32)
    plane[nlon * pitch : nlon * pitch + nlat, :] = forcing_ref[0].astype(f32)
    plane[(pitch - 1) * pitch : (pitch - 1) * pitch + nlat, :] = forcing_ref[nlon - 1].astype(f32)
    for j in range(nlat):
        state_a[RIM + j] = plane[pl.ds(j, pitch, stride=pitch), :]
    for side, first in ((0, nlat), (1, RIM)):
        rim_out[side] = jnp.concatenate(
            [
                state_a[first : first + RIM].reshape(RIM * pitch, species),
                jnp.zeros((rim_rows - RIM * pitch, species), f32),
            ],
            0,
        ).astype(bf16)

    pl.semaphore_wait(barrier, tiles + 1)

    def halo(side):
        place = t + 1 - 2 * side
        return (
            pltpu.make_async_remote_copy(
                src_ref=rim_out.at[side],
                dst_ref=rim_in.at[side],
                send_sem=halo_send.at[side],
                recv_sem=halo_recv.at[side],
                device_id=(level, place),
                device_id_type=MESH,
            ),
            pltpu.make_async_remote_copy(
                src_ref=weights_out.at[side],
                dst_ref=weights_rim.at[side],
                send_sem=rim_send.at[side],
                recv_sem=rim_recv.at[side],
                device_id=(level, place),
                device_id_type=MESH,
            ),
        )

    sends = [halo(0), halo(1)]

    @pl.when(t < tiles - 1)
    def _():
        for copy in sends[0]:
            copy.start()

    @pl.when(t > 0)
    def _():
        for copy in sends[1]:
            copy.start()

    @pl.when(t == 0)
    def _():
        rim_in[0] = jnp.zeros(rim_in.shape[1:], bf16)
        weights_rim[0] = jnp.zeros(weights_rim.shape[1:], f32)

    @pl.when(t == tiles - 1)
    def _():
        rim_in[1] = jnp.zeros(rim_in.shape[1:], bf16)
        weights_rim[1] = jnp.zeros(weights_rim.shape[1:], f32)

    mine = pl.ds(pl.multiple_of(t * owned, owned), owned)
    rate_copies = []
    for o in range(1, tiles):
        rate_copies.append(
            pltpu.make_async_remote_copy(
                src_ref=rates_own,
                dst_ref=rates_all.at[mine],
                send_sem=rate_send.at[o - 1],
                recv_sem=rate_recv.at[o - 1],
                device_id=(level, lax.rem(t + o, tiles)),
                device_id_type=MESH,
            )
        )
        rate_copies[-1].start()
    rates_all[mine, :] = rates_own[...]

    for j in range(nlat):
        weights[:, RIM + j] = jnp.broadcast_to(
            weights_own[:, :, j : j + 1], (5, pitch, species)
        )

    groups = pattern_ref.shape[0]
    width = species // groups
    member = (
        lax.broadcasted_iota(jnp.int32, (species, groups), 0) // width
        == lax.broadcasted_iota(jnp.int32, (species, groups), 1)
    ).astype(f32)
    mask = lax.dot_general(
        jnp.dot(member, pattern_ref[...].astype(f32), preferred_element_type=f32),
        member,
        (((1,), (1,)), ((), ())),
        preferred_element_type=f32,
    )
    coupling = jacobian_ref[...] * mask
    high = coupling.astype(bf16)
    low = (coupling - high.astype(f32)).astype(bf16)
    both = jnp.concatenate(
        [
            jnp.concatenate([high, low], 1),
            jnp.concatenate([high, jnp.zeros_like(low)], 1),
        ],
        0,
    )

    sums = [jnp.zeros((pitch, species), f32)] * 2

    def step(source, target, first, final, begin, end):
        chunk = GROUP if final else CHUNK
        for j0 in range(begin, end, chunk):
            n = min(chunk, end - j0)
            for j in range(j0, j0 + n, 2):
                here = source[j : j + 2]
                moved = (
                    here
                    + weights[0, j : j + 2] * (pltpu.roll(here, 1, 1) - here)
                    + weights[1, j : j + 2] * (pltpu.roll(here, pitch - 1, 1) - here)
                    + weights[2, j : j + 2] * (source[j - 1 : j + 1] - here)
                    + weights[3, j : j + 2] * (source[j + 1 : j + 3] - here)
                )
                moved = moved.reshape(2 * pitch, species)
                at = pl.ds((j - first) * pitch, 2 * pitch)
                moved_ref[at, :] = moved
                top = moved.astype(bf16)
                split_ref[at, 0:species] = top
                split_ref[at, species:] = (moved - top.astype(f32)).astype(bf16)
            at = pl.ds((j0 - first) * pitch, n * pitch)
            product = jnp.dot(split_ref[at, :], both, preferred_element_type=f32)
            reacted = product[:, :species] + product[:, species:]
            after = moved_ref[at, :].reshape(n, pitch, species) + weights[
                4, j0 : j0 + n
            ] * reacted.reshape(n, pitch, species)
            if final:
                rounded = after.reshape(n * pitch, species).astype(bf16)
                plane[at, :] = rounded.astype(f32)
                grad_out[at, :] = rounded
                grad_copies[(j0 - first) // GROUP].start()
                for j in range(j0 - first, j0 - first + n):
                    line = rounded[(j - j0 + first) * pitch : (j - j0 + first + 1) * pitch]
                    line = line.astype(f32)
                    sums[0] = sums[0] + to_north[j : j + 1] * line
                    sums[1] = sums[1] + to_south[j : j + 1] * line
            else:
                target[j0 : j0 + n] = after
                target[j0 : j0 + n, nlon : nlon + 1] = after[:, 0:1]
                target[j0 : j0 + n, pitch - 1 : pitch] = after[:, nlon - 1 : nlon]

    groups_at = [(k, min(GROUP, nlat - k)) for k in range(0, nlat, GROUP)]

    def rows_of(k):
        return pl.ds(groups_at[k][0] * pitch, groups_at[k][1] * pitch)

    grad_copies = [
        pltpu.make_async_remote_copy(
            src_ref=grad_out.at[rows_of(k)],
            dst_ref=grad_in.at[rows_of(k)],
            send_sem=grad_send.at[k],
            recv_sem=grad_recv.at[k],
            device_id=(across, t),
            device_id_type=MESH,
        )
        for k in range(len(groups_at))
    ]
    spare = pl.ds((nlat + 2) * pitch, (pitch - nlat - 2) * pitch)
    for buffer in (plane, plane_far):
        buffer[spare, :] = jnp.zeros(((pitch - nlat - 2) * pitch, species), f32)
    spare = pl.ds(nlon * pitch, (pitch - nlon) * pitch)
    for buffer in (lines_own, lines_far):
        buffer[spare, :] = jnp.zeros(((pitch - nlon) * pitch, species), f32)

    states = [state_a, state_b]
    low, top = 1, rows - 1
    step(state_a, state_b, low, False, low + RIM + 1, top - RIM - 1)

    @pl.when(t > 0)
    def _():
        sends[0][0].wait_recv()
        sends[0][1].wait_recv()

    @pl.when(t < tiles - 1)
    def _():
        sends[1][0].wait_recv()
        sends[1][1].wait_recv()

    for side, first in ((0, 0), (1, nlat + RIM)):
        rim = rim_in[side].astype(f32)[: RIM * pitch]
        state_a[first : first + RIM] = rim.reshape(RIM, pitch, species)
        for r in range(thin):
            for d in range(5):
                at = thin * d + r
                weights[d, (1, nlat + RIM)[side] + r] = jnp.broadcast_to(
                    weights_rim[side, :, at : at + 1], (pitch, species)
                )

    step(state_a, state_b, low, False, low, low + RIM + 1)
    step(state_a, state_b, low, False, top - RIM - 1, top)

    for copy in rate_copies:
        copy.wait()
    cell = lax.broadcasted_iota(jnp.int32, (pitch, rate_width), 1)
    row = lax.broadcasted_iota(jnp.int32, (pitch, rate_width), 0)
    start = t * nlat
    lat_cell = cell < lat_total
    picks = jnp.concatenate(
        [
            (cell == start + row) & (row < nlat),
            (cell >= start) & (cell <= start + row) & (cell < start + nlat),
            (cell < row * nlat) & lat_cell,
            (cell == lon_at + row) & (row < nlon),
        ],
        0,
    ).astype(f32)
    lines = lax.dot_general(
        picks,
        rates_all[...],
        (((1,), (1,)), ((), ())),
        precision=HIGHEST,
        preferred_element_type=f32,
    )
    lat_line = lines[0:pitch]
    lat_sum = lines[pitch : 2 * pitch]
    before = lines[2 * pitch : 3 * pitch]
    lon_line = lines[3 * pitch :]
    lat_q, lat_d = jnp.sqrt(jnp.sqrt(lat_line)), jnp.exp(-lat_line)
    lon_q, lon_d = jnp.sqrt(jnp.sqrt(lon_line)), jnp.exp(-lon_line)

    to_north = lat_q * jnp.exp(lat_sum - lat_sum[nlat - 1 : nlat])
    to_south = lat_q * jnp.exp(-lat_sum)

    for sweep in range(1, STEPS):
        step(
            states[sweep % 2],
            states[(sweep + 1) % 2],
            1 + sweep,
            sweep == STEPS - 1,
            1 + sweep,
            rows - 1 - sweep,
        )
    carry_out[0] = sums[0]
    carry_out[1] = sums[1]

    carry_copies = []
    for o in range(1, tiles):
        carry_copies.append(
            pltpu.make_async_remote_copy(
                src_ref=carry_out.at[(t + o) // tiles],
                dst_ref=carry_in.at[o - 1],
                send_sem=carry_send.at[o - 1],
                recv_sem=carry_recv.at[o - 1],
                device_id=(level, lax.rem(t + o, tiles)),
                device_id_type=MESH,
            )
        )
        carry_copies[-1].start()

    def along_lon(source, target, first, n):
        def item(i):
            cells = source[pl.ds(first * pitch + i, n, stride=pitch), :]
            return lon_q[i : i + 1] * cells

        carry = jnp.zeros((n, species), f32)
        for i in range(nlon):
            carry = item(i) + lon_d[i : i + 1] * carry
            target[pl.ds(i * pitch + first, n), :] = carry
        later = jnp.zeros((n, species), f32)
        for i in range(nlon - 1, -1, -1):
            at = pl.ds(i * pitch + first, n)
            target[at, :] = lon_q[i : i + 1] * (target[at, :] + later)
            later = lon_d[i : i + 1] * (item(i) + later)

    def take(k):
        grad_copies[k].wait_recv()
        plane_far[rows_of(k), :] = grad_in[rows_of(k), :].astype(f32)

    split_at = len(groups_at) - 2
    along_lon(plane, lines_own, 0, (len(groups_at) - 1) * GROUP)
    for begin, end in ((0, split_at - 1), (split_at - 1, split_at)):
        for k in range(begin, end):
            take(k)
        along_lon(plane_far, lines_far, begin * GROUP, (end - begin) * GROUP)

    order = lax.broadcasted_iota(jnp.int32, (pitch, species), 0)

    def before_tile(u):
        return jnp.sum(jnp.where(order == u, before, 0.0), 0, keepdims=True)

    south = jnp.zeros((pitch, species), f32)
    north = jnp.zeros((pitch, species), f32)
    for o in range(1, tiles):
        u = lax.rem(t + tiles - o, tiles)
        upper, lower = jnp.maximum(u, t), jnp.minimum(u, t)
        factor = jnp.exp(before_tile(lower + 1) - before_tile(upper))
        carry_copies[o - 1].wait()
        term = factor * carry_in[o - 1]
        south = south + jnp.where(o <= t, term, 0.0)
        north = north + jnp.where(o <= t, 0.0, term)
    plane[nlat * pitch : (nlat + 1) * pitch, :] = south
    plane[(nlat + 1) * pitch : (nlat + 2) * pitch, :] = north
    carried = pl.ds(nlat * pitch, 2 * pitch)
    both_copy = pltpu.make_async_remote_copy(
        src_ref=plane.at[carried],
        dst_ref=plane_far.at[carried],
        send_sem=both_send,
        recv_sem=both_recv,
        device_id=(across, t),
        device_id_type=MESH,
    )
    both_copy.start()

    def along_lat(lines_ref, slot):
        def line(j):
            return lines_ref[pl.ds(j, pitch, stride=pitch), :]

        carry = line(nlat)
        for j in range(nlat):
            carry = lat_q[j : j + 1] * line(j) + lat_d[j : j + 1] * carry
            ahead_ref[j] = carry
        later = line(nlat + 1)
        copies = {}
        for k in range(len(groups_at) - 1, -1, -1):
            first, n = groups_at[k]
            for j in range(first + n - 2, first - 1, -2):
                done = []
                for row_at in (j + 1, j):
                    q = lat_q[row_at : row_at + 1]
                    done.append(q * (ahead_ref[row_at] + later))
                    later = lat_d[row_at : row_at + 1] * (q * line(row_at) + later)
                fields[slot, pl.ds(j * pitch, 2 * pitch), :] = jnp.concatenate(
                    done[::-1], 0
                ).astype(bf16)
            copies[k] = pltpu.make_async_remote_copy(
                src_ref=fields.at[slot, rows_of(k)],
                dst_ref=fields.at[slot + 1, rows_of(k)],
                send_sem=level_send.at[slot // 2, k],
                recv_sem=level_recv.at[slot // 2, k],
                device_id=(sibling, t),
                device_id_type=MESH,
            )
            copies[k].start()
        return copies

    last_group = len(groups_at) - 1
    along_lon(plane, lines_own, last_group * GROUP, pitch - last_group * GROUP)
    near = along_lat(lines_own, 0)
    for k in range(split_at, len(groups_at)):
        take(k)
    both_copy.wait_recv()
    along_lon(plane_far, lines_far, split_at * GROUP, pitch - split_at * GROUP)
    relay = along_lat(lines_far, 2)

    loads[-1].wait()
    factors = [
        vertical_ref[level, pl.ds(source, 1), :]
        for source in (level, sibling, across, lax.rem(sibling + 2, levels))
    ]
    scale = step_scale_ref[...]
    for k in range(last_group, -1, -1):
        near[k].wait_recv()
        relay[k].wait_recv()
        at = rows_of(k)
        total = factors[0] * fields[0, at, :].astype(f32)
        for slot in range(1, levels):
            total = total + factors[slot] * fields[slot, at, :].astype(f32)
        moved_ref[at, :] = scale * total
    for i in range(nlon):
        total = moved_ref[pl.ds(i, pitch, stride=pitch), :]
        out_ref[i] = (control_ref[i].astype(f32) - total[:nlat]).astype(bf16)
    @pl.when(t < tiles - 1)
    def _():
        sends[0][0].wait_send()
        sends[0][1].wait_send()

    @pl.when(t > 0)
    def _():
        sends[1][0].wait_send()
        sends[1][1].wait_send()

    both_copy.wait_send()
    for k in range(len(groups_at)):
        grad_copies[k].wait_send()
        near[k].wait_send()
        relay[k].wait_send()


def on_device_fused(
    tiles,
    levels,
    forcing,
    transport,
    reactivity,
    jacobian,
    pattern,
    lon_rate,
    lat_rate,
    vertical,
    step_scale,
    control,
):
    nlon, nlat, species = forcing.shape[2:]
    pitch = up_to(max(nlon + 2, nlat), 8)
    rows = nlat + 2 * RIM
    owned, lat_total = lat_rate.shape
    rate_width = up_to(lat_total + nlon, 128)
    f32, bf16 = jnp.float32, jnp.bfloat16
    dma = pltpu.SemaphoreType.DMA
    count = -(-nlat // GROUP)
    rim_rows = up_to(RIM * pitch, 16)
    inputs = (
        forcing[0, 0],
        transport[:, 0, 0][:, :, None],
        reactivity[0, 0][:, None],
        jacobian[0],
        pattern,
        lon_rate,
        lat_rate,
        jnp.transpose(vertical, (1, 2, 0)),
        step_scale[None],
        control[0, 0],
    )
    updated = pl.pallas_call(
        functools.partial(fused_kernel, tiles, levels),
        out_shape=jax.ShapeDtypeStruct((nlon, nlat, species), bf16),
        in_specs=[pl.BlockSpec(memory_space=pltpu.HBM)] * 10,
        out_specs=pl.BlockSpec(memory_space=pltpu.VMEM),
        scratch_shapes=[pltpu.VMEM(x.shape, x.dtype) for x in inputs]
        + [
            dma((len(inputs),)),
            pltpu.VMEM((rows, pitch, species), f32),
            pltpu.VMEM((rows, pitch, species), f32),
            pltpu.VMEM((5, pitch, 128), f32),
            pltpu.VMEM((2, pitch, 128), f32),
            pltpu.VMEM((2, pitch, 128), f32),
            pltpu.VMEM((2, rim_rows, species), bf16),
            pltpu.VMEM((2, rim_rows, species), bf16),
            pltpu.VMEM((5, rows, pitch, species), f32),
            pltpu.VMEM((rows * pitch, species), f32),
            pltpu.VMEM((rows * pitch, 2 * species), bf16),
            pltpu.VMEM((pitch * pitch, species), f32),
            pltpu.VMEM((pitch, pitch, species), f32),
            pltpu.VMEM((owned, rate_width), f32),
            pltpu.VMEM((species, rate_width), f32),
            pltpu.VMEM((2, pitch, species), f32),
            pltpu.VMEM((tiles - 1, pitch, species), f32),
            pltpu.VMEM((pitch * pitch, species), f32),
            pltpu.VMEM((pitch * pitch, species), f32),
            pltpu.VMEM((pitch * pitch, species), f32),
            pltpu.VMEM((nlat * pitch, species), bf16),
            pltpu.VMEM((nlat * pitch, species), bf16),
            pltpu.VMEM((levels, nlat * pitch, species), bf16),
            dma((2,)),
            dma((2,)),
            dma((2,)),
            dma((2,)),
            dma((tiles - 1,)),
            dma((tiles - 1,)),
            dma((tiles - 1,)),
            dma((tiles - 1,)),
            dma((count,)),
            dma((count,)),
            dma,
            dma,
            dma((2, count)),
            dma((2, count)),
        ],
        compiler_params=pltpu.CompilerParams(
            collective_id=0, has_side_effects=True, vmem_limit_bytes=54500 * 1024
        ),
        name="fused",
    )(*inputs)
    return updated[None, None]


def on_device(forcing, *others):
    tiles, levels = lax.axis_size("tile"), lax.axis_size("lev")
    nlon, nlat, species = forcing.shape[2:]
    one_ring = tiles == TJ and levels == 4
    fits = nlon == nlat and nlat % GROUP in (2, 4) and nlat > 3 * GROUP and nlat + 2 * RIM <= 128
    if one_ring and fits and species == 128:
        return on_device_fused(tiles, levels, forcing, *others)
    return on_device_general(forcing, *others)


def solution(mesh):
    in_specs = (
        P("lev", "tile", None, None, None),
        P(None, "lev", "tile", None, None),
        P("lev", "tile", None, None),
        P("lev", None, None),
        P(),
        P("tile", None),
        P("tile", None),
        P(),
        P(),
        P("lev", "tile", None, None, None),
    )
    out_specs = P("lev", "tile", None, None, None)
    return jax.shard_map(
        on_device, mesh=mesh, in_specs=in_specs, out_specs=out_specs, check_vma=False
    )
```

```python
import functools

import jax
import jax.numpy as jnp
from jax import lax
from jax.experimental import pallas as pl
from jax.experimental.pallas import tpu as pltpu
from jax.sharding import PartitionSpec as P

TJ = 8
STEPS = 3


HIGHEST = lax.Precision.HIGHEST


def from_behind(x, axis, by):
    size = lax.axis_size(axis)
    return lax.ppermute(x, axis, [(i, (i + by) % size) for i in range(size)])


def neighbour_rim(edge, offset):
    return from_behind(edge, "tile", offset)


def filter_kernel(rates, blocks):
    cumulative = jnp.cumsum(rates)
    quarter = jnp.sqrt(jnp.sqrt(rates))
    kernel = (
        quarter[:, None]
        * quarter[None, :]
        * jnp.exp(-jnp.abs(cumulative[:, None] - cumulative[None, :]))
    )
    length = rates.shape[0] // blocks
    return kernel.reshape(blocks, length, blocks, length)


def on_device_general(
    forcing,
    transport,
    reactivity,
    jacobian,
    pattern,
    lon_rate,
    lat_rate,
    vertical,
    step_scale,
    control,
):
    adjoint = forcing[0, 0].astype(jnp.float32)
    tile_rows, tile_cols, species = adjoint.shape
    weights = transport[:, 0, 0]
    reacting = reactivity[0, 0][:, :, None]
    groups = pattern.shape[0]
    width = species // groups
    blockmask = jnp.broadcast_to(
        pattern.astype(jnp.float32)[:, None, :, None], (groups, width, groups, width)
    ).reshape(species, species)
    coupling = jacobian[0] * blockmask
    tiles = lax.axis_size("tile")
    lon_tiles = tiles // TJ
    placing = lax.axis_index("tile") % TJ
    keep_south = (placing > 0).astype(jnp.float32)
    keep_north = (placing < TJ - 1).astype(jnp.float32)
    for sweep in range(STEPS):
        if lon_tiles > 1:
            west_rim = neighbour_rim(adjoint[-1], TJ)
            east_rim = neighbour_rim(adjoint[0], -TJ)
        else:
            west_rim = adjoint[-1]
            east_rim = adjoint[0]
        south_rim = neighbour_rim(adjoint[:, -1], 1) * keep_south
        north_rim = neighbour_rim(adjoint[:, 0], -1) * keep_north
        from_west = jnp.concatenate([west_rim[None], adjoint[:-1]], 0)
        from_east = jnp.concatenate([adjoint[1:], east_rim[None]], 0)
        from_south = jnp.concatenate([south_rim[:, None], adjoint[:, :-1]], 1)
        from_north = jnp.concatenate([adjoint[:, 1:], north_rim[:, None]], 1)
        moved = (
            adjoint
            + weights[0][:, :, None] * (from_west - adjoint)
            + weights[1][:, :, None] * (from_east - adjoint)
            + weights[2][:, :, None] * (from_south - adjoint)
            + weights[3][:, :, None] * (from_north - adjoint)
        )
        reacted = jnp.dot(
            moved.reshape(tile_rows * tile_cols, species),
            coupling,
            precision=HIGHEST,
            preferred_element_type=jnp.float32,
        )
        adjoint = moved + reacting * reacted.reshape(tile_rows, tile_cols, species)
    gradient = adjoint.astype(jnp.bfloat16)
    planes = lax.all_to_all(
        gradient.reshape(1, tile_rows * tile_cols, species),
        "tile",
        split_axis=2,
        concat_axis=0,
        tiled=True,
    )
    owned = planes.shape[2]
    planes = jnp.moveaxis(planes.reshape(lon_tiles, TJ, tile_rows, tile_cols, owned), 4, 0)

    def filter_species(inputs):
        lon_line, lat_line, plane = inputs
        lon_kernel = filter_kernel(lon_line, lon_tiles)
        lat_kernel = filter_kernel(lat_line, TJ)
        along_lon = jnp.einsum(
            "abcd,cjdy->ajby", lon_kernel, plane.astype(jnp.float32), precision=HIGHEST
        )
        return jnp.einsum("jykz,akbz->ajby", lat_kernel, along_lon, precision=HIGHEST).astype(
            jnp.bfloat16
        )

    filtered = jnp.moveaxis(lax.map(filter_species, (lon_rate, lat_rate, planes)), 0, 4)
    level_here = lax.axis_index("lev")
    mixing = lax.dynamic_index_in_dim(vertical, level_here, 1, keepdims=False)
    returned = lax.all_to_all(
        filtered.reshape(tiles, tile_rows * tile_cols, owned),
        "tile",
        split_axis=0,
        concat_axis=2,
        tiled=True,
    )
    factor = mixing.T
    summed = jnp.sum(
        lax.all_gather(returned, "lev", axis=0, tiled=True) * factor[:, None, :], axis=0
    )
    increment = summed.reshape(tile_rows, tile_cols, species)
    updated = control[0, 0].astype(jnp.float32) - step_scale * increment
    return updated.astype(jnp.bfloat16)[None, None]


MESH = pl.DeviceIdType.MESH
RIM = STEPS
CHUNK = 10
GROUP = 8


def up_to(size, multiple):
    return -(-size // multiple) * multiple


def fused_kernel(tiles, levels, *refs):
    inputs, out_ref, held, arrived = refs[:10], refs[10], refs[11:21], refs[21]
    (
        forcing_ref,
        transport_ref,
        reactivity_ref,
        jacobian_ref,
        pattern_ref,
        lon_rate_ref,
        lat_rate_ref,
        vertical_ref,
        step_scale_ref,
        control_ref,
    ) = held
    (
        state_a,
        state_b,
        weights_own,
        weights_out,
        weights_rim,
        rim_out,
        rim_in,
        weights,
        moved_ref,
        split_ref,
        plane,
        ahead_ref,
        rates_own,
        rates_all,
        carry_out,
        carry_in,
        plane_far,
        lines_own,
        lines_far,
        grad_out,
        grad_in,
        fields,
        halo_send,
        halo_recv,
        rim_send,
        rim_recv,
        rate_send,
        rate_recv,
        carry_send,
        carry_recv,
        grad_send,
        grad_recv,
        both_send,
        both_recv,
        level_send,
        level_recv,
    ) = refs[22:]
    loads = [
        pltpu.make_async_copy(source, target, arrived.at[k])
        for k, (source, target) in enumerate(zip(inputs, held))
    ]
    for load in loads:
        load.start()
    nlon, nlat, species = forcing_ref.shape
    pitch = state_a.shape[1]
    rows = nlat + 2 * RIM
    rim_rows = rim_out.shape[1]
    owned, lat_total = lat_rate_ref.shape
    lon_at = nlat
    sums_at = nlat + nlon
    rate_width = rates_own.shape[2]
    t = lax.axis_index("tile")
    level = lax.axis_index("lev")
    sibling = level + 1 - 2 * lax.rem(level, 2)
    across = lax.rem(level + 2, levels)
    f32, bf16 = jnp.float32, jnp.bfloat16

    barrier = pltpu.get_barrier_semaphore()
    for o in range(1, tiles):
        pl.semaphore_signal(
            barrier, inc=1, device_id=(level, lax.rem(t + o, tiles)), device_id_type=MESH
        )
    for other in (sibling, across):
        pl.semaphore_signal(barrier, inc=1, device_id=(other, t), device_id_type=MESH)

    weights_own[...] = jnp.zeros_like(weights_own)
    plane[...] = jnp.zeros_like(plane)
    for load in loads[:-1]:
        load.wait()
    weights_own[0:4, 0:nlon, 0:nlat] = transport_ref[...].reshape(4, nlon, nlat)
    weights_own[4, 0:nlon, 0:nlat] = reactivity_ref[...].reshape(nlon, nlat)
    lane = lax.broadcasted_iota(jnp.int32, (pitch, 128), 1)
    thin = RIM - 1
    for side, first in ((0, nlat - thin), (1, 0)):
        packed = jnp.zeros((pitch, 128), f32)
        for d in range(5):
            moved_lanes = pltpu.roll(weights_own[d], (thin * d - first) % 128, 1)
            packed = jnp.where(lane // thin == d, moved_lanes, packed)
        weights_out[side] = packed
    rate_lane = lax.broadcasted_iota(jnp.int32, (owned, rate_width), 1)
    running = jnp.zeros((owned, 1), f32)
    sums_of = jnp.zeros((owned, rate_width), f32)
    for u in range(tiles):
        running = running + jnp.sum(
            lat_rate_ref[:, u * nlat : (u + 1) * nlat], 1, keepdims=True
        )
        sums_of = jnp.where(rate_lane == sums_at + u + 1, running, sums_of)
    for u in range(tiles):
        rates_own[u] = sums_of
        rates_own[u, :, 0:nlat] = lat_rate_ref[:, u * nlat : (u + 1) * nlat]
        rates_own[u, :, lon_at : lon_at + nlon] = lon_rate_ref[...]
    for i in range(nlon):
        plane[i * pitch : i * pitch + nlat, :] = forcing_ref[i].astype(f32)
    plane[nlon * pitch : nlon * pitch + nlat, :] = forcing_ref[0].astype(f32)
    plane[(pitch - 1) * pitch : (pitch - 1) * pitch + nlat, :] = forcing_ref[nlon - 1].astype(f32)
    for j in range(nlat):
        state_a[RIM + j] = plane[pl.ds(j, pitch, stride=pitch), :]
    for side, first in ((0, nlat), (1, RIM)):
        rim_out[side] = jnp.concatenate(
            [
                state_a[first : first + RIM].reshape(RIM * pitch, species),
                jnp.zeros((rim_rows - RIM * pitch, species), f32),
            ],
            0,
        ).astype(bf16)

    pl.semaphore_wait(barrier, tiles + 1)

    def halo(side):
        place = t + 1 - 2 * side
        return (
            pltpu.make_async_remote_copy(
                src_ref=rim_out.at[side],
                dst_ref=rim_in.at[side],
                send_sem=halo_send.at[side],
                recv_sem=halo_recv.at[side],
                device_id=(level, place),
                device_id_type=MESH,
            ),
            pltpu.make_async_remote_copy(
                src_ref=weights_out.at[side],
                dst_ref=weights_rim.at[side],
                send_sem=rim_send.at[side],
                recv_sem=rim_recv.at[side],
                device_id=(level, place),
                device_id_type=MESH,
            ),
        )

    sends = [halo(0), halo(1)]

    @pl.when(t < tiles - 1)
    def _():
        for copy in sends[0]:
            copy.start()

    @pl.when(t > 0)
    def _():
        for copy in sends[1]:
            copy.start()

    @pl.when(t == 0)
    def _():
        rim_in[0] = jnp.zeros(rim_in.shape[1:], bf16)
        weights_rim[0] = jnp.zeros(weights_rim.shape[1:], f32)

    @pl.when(t == tiles - 1)
    def _():
        rim_in[1] = jnp.zeros(rim_in.shape[1:], bf16)
        weights_rim[1] = jnp.zeros(weights_rim.shape[1:], f32)

    mine = pl.ds(pl.multiple_of(t * owned, owned), owned)
    rate_copies = []
    for o in range(1, tiles):
        rate_copies.append(
            pltpu.make_async_remote_copy(
                src_ref=rates_own.at[lax.rem(t + o, tiles)],
                dst_ref=rates_all.at[mine],
                send_sem=rate_send.at[o - 1],
                recv_sem=rate_recv.at[o - 1],
                device_id=(level, lax.rem(t + o, tiles)),
                device_id_type=MESH,
            )
        )
        rate_copies[-1].start()
    rates_all[mine, :] = rates_own[t]

    for j in range(nlat):
        weights[:, RIM + j] = jnp.broadcast_to(
            weights_own[:, :, j : j + 1], (5, pitch, species)
        )

    groups = pattern_ref.shape[0]
    width = species // groups
    member = (
        lax.broadcasted_iota(jnp.int32, (species, groups), 0) // width
        == lax.broadcasted_iota(jnp.int32, (species, groups), 1)
    ).astype(f32)
    mask = lax.dot_general(
        jnp.dot(member, pattern_ref[...].astype(f32), preferred_element_type=f32),
        member,
        (((1,), (1,)), ((), ())),
        preferred_element_type=f32,
    )
    coupling = jacobian_ref[...] * mask
    high = coupling.astype(bf16)
    low = (coupling - high.astype(f32)).astype(bf16)
    both = jnp.concatenate(
        [
            jnp.concatenate([high, low], 1),
            jnp.concatenate([high, jnp.zeros_like(low)], 1),
        ],
        0,
    )

    sums = [jnp.zeros((pitch, species), f32)] * 2

    def step(source, target, first, final, begin, end):
        chunk = GROUP if final else CHUNK
        for j0 in range(begin, end, chunk):
            n = min(chunk, end - j0)
            for j in range(j0, j0 + n, 2):
                here = source[j : j + 2]
                moved = (
                    here
                    + weights[0, j : j + 2] * (pltpu.roll(here, 1, 1) - here)
                    + weights[1, j : j + 2] * (pltpu.roll(here, pitch - 1, 1) - here)
                    + weights[2, j : j + 2] * (source[j - 1 : j + 1] - here)
                    + weights[3, j : j + 2] * (source[j + 1 : j + 3] - here)
                )
                moved = moved.reshape(2 * pitch, species)
                at = pl.ds((j - first) * pitch, 2 * pitch)
                moved_ref[at, :] = moved
                top = moved.astype(bf16)
                split_ref[at, 0:species] = top
                split_ref[at, species:] = (moved - top.astype(f32)).astype(bf16)
            at = pl.ds((j0 - first) * pitch, n * pitch)
            product = jnp.dot(split_ref[at, :], both, preferred_element_type=f32)
            reacted = product[:, :species] + product[:, species:]
            after = moved_ref[at, :].reshape(n, pitch, species) + weights[
                4, j0 : j0 + n
            ] * reacted.reshape(n, pitch, species)
            if final:
                rounded = after.reshape(n * pitch, species).astype(bf16)
                plane[at, :] = rounded.astype(f32)
                grad_out[at, :] = rounded
                grad_copies[(j0 - first) // GROUP].start()
                for j in range(j0 - first, j0 - first + n):
                    line = rounded[(j - j0 + first) * pitch : (j - j0 + first + 1) * pitch]
                    line = line.astype(f32)
                    sums[0] = sums[0] + to_north[j : j + 1] * line
                    sums[1] = sums[1] + to_south[j : j + 1] * line
            else:
                target[j0 : j0 + n] = after
                target[j0 : j0 + n, nlon : nlon + 1] = after[:, 0:1]
                target[j0 : j0 + n, pitch - 1 : pitch] = after[:, nlon - 1 : nlon]

    groups_at = [(k, min(GROUP, nlat - k)) for k in range(0, nlat, GROUP)]

    def rows_of(k):
        return pl.ds(groups_at[k][0] * pitch, groups_at[k][1] * pitch)

    grad_copies = [
        pltpu.make_async_remote_copy(
            src_ref=grad_out.at[rows_of(k)],
            dst_ref=grad_in.at[rows_of(k)],
            send_sem=grad_send.at[k],
            recv_sem=grad_recv.at[k],
            device_id=(across, t),
            device_id_type=MESH,
        )
        for k in range(len(groups_at))
    ]
    spare = pl.ds((nlat + 2) * pitch, (pitch - nlat - 2) * pitch)
    for buffer in (plane, plane_far):
        buffer[spare, :] = jnp.zeros(((pitch - nlat - 2) * pitch, species), f32)
    spare = pl.ds(nlon * pitch, (pitch - nlon) * pitch)
    for buffer in (lines_own, lines_far):
        buffer[spare, :] = jnp.zeros(((pitch - nlon) * pitch, species), f32)

    states = [state_a, state_b]
    low, top = 1, rows - 1
    step(state_a, state_b, low, False, low + RIM + 1, top - RIM - 1)

    @pl.when(t > 0)
    def _():
        sends[0][0].wait_recv()
        sends[0][1].wait_recv()

    @pl.when(t < tiles - 1)
    def _():
        sends[1][0].wait_recv()
        sends[1][1].wait_recv()

    for side, first in ((0, 0), (1, nlat + RIM)):
        rim = rim_in[side].astype(f32)[: RIM * pitch]
        state_a[first : first + RIM] = rim.reshape(RIM, pitch, species)
        for r in range(thin):
            for d in range(5):
                at = thin * d + r
                weights[d, (1, nlat + RIM)[side] + r] = jnp.broadcast_to(
                    weights_rim[side, :, at : at + 1], (pitch, species)
                )

    step(state_a, state_b, low, False, low, low + RIM + 1)
    step(state_a, state_b, low, False, top - RIM - 1, top)

    last_sweep = STEPS - 1
    for sweep in range(1, last_sweep):
        step(
            states[sweep % 2],
            states[(sweep + 1) % 2],
            1 + sweep,
            False,
            1 + sweep,
            rows - 1 - sweep,
        )

    for copy in rate_copies:
        copy.wait()
    cell = lax.broadcasted_iota(jnp.int32, (pitch, rate_width), 1)
    row = lax.broadcasted_iota(jnp.int32, (pitch, rate_width), 0)
    picks = jnp.concatenate(
        [
            (cell == row) & (row < nlat),
            (cell <= row) & (cell < nlat),
            (cell == sums_at + row) & (row <= tiles),
            (cell == lon_at + row) & (row < nlon),
        ],
        0,
    ).astype(f32)
    lines = lax.dot_general(
        picks,
        rates_all[...],
        (((1,), (1,)), ((), ())),
        precision=HIGHEST,
        preferred_element_type=f32,
    )
    lat_line = lines[0:pitch]
    lat_sum = lines[pitch : 2 * pitch]
    before = lines[2 * pitch : 3 * pitch]
    lon_line = lines[3 * pitch :]
    lat_q, lat_d = jnp.sqrt(jnp.sqrt(lat_line)), jnp.exp(-lat_line)
    lon_q, lon_d = jnp.sqrt(jnp.sqrt(lon_line)), jnp.exp(-lon_line)

    to_north = lat_q * jnp.exp(lat_sum - lat_sum[nlat - 1 : nlat])
    to_south = lat_q * jnp.exp(-lat_sum)

    step(
        states[last_sweep % 2],
        None,
        1 + last_sweep,
        True,
        1 + last_sweep,
        rows - 1 - last_sweep,
    )
    carry_out[0] = sums[0]
    carry_out[1] = sums[1]

    carry_copies = []
    for o in range(1, tiles):
        carry_copies.append(
            pltpu.make_async_remote_copy(
                src_ref=carry_out.at[(t + o) // tiles],
                dst_ref=carry_in.at[o - 1],
                send_sem=carry_send.at[o - 1],
                recv_sem=carry_recv.at[o - 1],
                device_id=(level, lax.rem(t + o, tiles)),
                device_id_type=MESH,
            )
        )
        carry_copies[-1].start()

    def along_lon(source, target, first, n):
        def item(i):
            cells = source[pl.ds(first * pitch + i, n, stride=pitch), :]
            return lon_q[i : i + 1] * cells

        carry = jnp.zeros((n, species), f32)
        for i in range(nlon):
            carry = item(i) + lon_d[i : i + 1] * carry
            target[pl.ds(i * pitch + first, n), :] = carry
        later = jnp.zeros((n, species), f32)
        for i in range(nlon - 1, -1, -1):
            at = pl.ds(i * pitch + first, n)
            target[at, :] = lon_q[i : i + 1] * (target[at, :] + later)
            later = lon_d[i : i + 1] * (item(i) + later)

    def take(k):
        grad_copies[k].wait_recv()
        plane_far[rows_of(k), :] = grad_in[rows_of(k), :].astype(f32)

    split_at = len(groups_at) - 2
    along_lon(plane, lines_own, 0, (len(groups_at) - 1) * GROUP)
    for begin, end in ((0, split_at - 1), (split_at - 1, split_at)):
        for k in range(begin, end):
            take(k)
        along_lon(plane_far, lines_far, begin * GROUP, (end - begin) * GROUP)

    order = lax.broadcasted_iota(jnp.int32, (pitch, species), 0)

    def before_tile(u):
        return jnp.sum(jnp.where(order == u, before, 0.0), 0, keepdims=True)

    south = jnp.zeros((pitch, species), f32)
    north = jnp.zeros((pitch, species), f32)
    for o in range(1, tiles):
        u = lax.rem(t + tiles - o, tiles)
        upper, lower = jnp.maximum(u, t), jnp.minimum(u, t)
        factor = jnp.exp(before_tile(lower + 1) - before_tile(upper))
        carry_copies[o - 1].wait()
        term = factor * carry_in[o - 1]
        south = south + jnp.where(o <= t, term, 0.0)
        north = north + jnp.where(o <= t, 0.0, term)
    plane[nlat * pitch : (nlat + 1) * pitch, :] = south
    plane[(nlat + 1) * pitch : (nlat + 2) * pitch, :] = north
    carried = pl.ds(nlat * pitch, 2 * pitch)
    both_copy = pltpu.make_async_remote_copy(
        src_ref=plane.at[carried],
        dst_ref=plane_far.at[carried],
        send_sem=both_send,
        recv_sem=both_recv,
        device_id=(across, t),
        device_id_type=MESH,
    )
    both_copy.start()

    def along_lat(lines_ref, slot):
        def line(j):
            return lines_ref[pl.ds(j, pitch, stride=pitch), :]

        carry = line(nlat)
        for j in range(nlat):
            carry = lat_q[j : j + 1] * line(j) + lat_d[j : j + 1] * carry
            ahead_ref[j] = carry
        later = line(nlat + 1)
        copies = {}
        for k in range(len(groups_at) - 1, -1, -1):
            first, n = groups_at[k]
            for j in range(first + n - 2, first - 1, -2):
                done = []
                for row_at in (j + 1, j):
                    q = lat_q[row_at : row_at + 1]
                    done.append(q * (ahead_ref[row_at] + later))
                    later = lat_d[row_at : row_at + 1] * (q * line(row_at) + later)
                fields[slot, pl.ds(j * pitch, 2 * pitch), :] = jnp.concatenate(
                    done[::-1], 0
                ).astype(bf16)
            copies[k] = pltpu.make_async_remote_copy(
                src_ref=fields.at[slot, rows_of(k)],
                dst_ref=fields.at[slot + 1, rows_of(k)],
                send_sem=level_send.at[slot // 2, k],
                recv_sem=level_recv.at[slot // 2, k],
                device_id=(sibling, t),
                device_id_type=MESH,
            )
            copies[k].start()
        return copies

    last_group = len(groups_at) - 1
    along_lon(plane, lines_own, last_group * GROUP, pitch - last_group * GROUP)
    near = along_lat(lines_own, 0)
    for k in range(split_at, len(groups_at)):
        take(k)
    both_copy.wait_recv()
    along_lon(plane_far, lines_far, split_at * GROUP, pitch - split_at * GROUP)
    relay = along_lat(lines_far, 2)

    loads[-1].wait()
    factors = [
        vertical_ref[level, pl.ds(source, 1), :]
        for source in (level, sibling, across, lax.rem(sibling + 2, levels))
    ]
    scale = step_scale_ref[...]
    for k in range(last_group, -1, -1):
        near[k].wait_recv()
        relay[k].wait_recv()
        at = rows_of(k)
        total = factors[0] * fields[0, at, :].astype(f32)
        for slot in range(1, levels):
            total = total + factors[slot] * fields[slot, at, :].astype(f32)
        moved_ref[at, :] = scale * total
    for i in range(nlon):
        total = moved_ref[pl.ds(i, pitch, stride=pitch), :]
        out_ref[i] = control_ref[i].astype(f32) - total[:nlat]
    @pl.when(t < tiles - 1)
    def _():
        sends[0][0].wait_send()
        sends[0][1].wait_send()

    @pl.when(t > 0)
    def _():
        sends[1][0].wait_send()
        sends[1][1].wait_send()

    both_copy.wait_send()
    for k in range(len(groups_at)):
        grad_copies[k].wait_send()
        near[k].wait_send()
        relay[k].wait_send()


def on_device_fused(
    tiles,
    levels,
    forcing,
    transport,
    reactivity,
    jacobian,
    pattern,
    lon_rate,
    lat_rate,
    vertical,
    step_scale,
    control,
):
    nlon, nlat, species = forcing.shape[2:]
    pitch = up_to(max(nlon + 2, nlat), 8)
    rows = nlat + 2 * RIM
    owned, lat_total = lat_rate.shape
    rate_width = up_to(nlat + nlon + tiles + 1, 128)
    f32, bf16 = jnp.float32, jnp.bfloat16
    dma = pltpu.SemaphoreType.DMA
    count = -(-nlat // GROUP)
    rim_rows = up_to(RIM * pitch, 16)
    inputs = (
        forcing[0, 0],
        transport[:, 0, 0][:, :, None],
        reactivity[0, 0][:, None],
        jacobian[0],
        pattern,
        lon_rate,
        lat_rate,
        jnp.transpose(vertical, (1, 2, 0)),
        step_scale[None],
        control[0, 0],
    )
    updated = pl.pallas_call(
        functools.partial(fused_kernel, tiles, levels),
        out_shape=jax.ShapeDtypeStruct((nlon, nlat, species), f32),
        in_specs=[pl.BlockSpec(memory_space=pltpu.HBM)] * 10,
        out_specs=pl.BlockSpec(memory_space=pltpu.VMEM),
        scratch_shapes=[pltpu.VMEM(x.shape, x.dtype) for x in inputs]
        + [
            dma((len(inputs),)),
            pltpu.VMEM((rows, pitch, species), f32),
            pltpu.VMEM((rows, pitch, species), f32),
            pltpu.VMEM((5, pitch, 128), f32),
            pltpu.VMEM((2, pitch, 128), f32),
            pltpu.VMEM((2, pitch, 128), f32),
            pltpu.VMEM((2, rim_rows, species), bf16),
            pltpu.VMEM((2, rim_rows, species), bf16),
            pltpu.VMEM((5, rows, pitch, species), f32),
            pltpu.VMEM((rows * pitch, species), f32),
            pltpu.VMEM((rows * pitch, 2 * species), bf16),
            pltpu.VMEM((pitch * pitch, species), f32),
            pltpu.VMEM((pitch, pitch, species), f32),
            pltpu.VMEM((tiles, owned, rate_width), f32),
            pltpu.VMEM((species, rate_width), f32),
            pltpu.VMEM((2, pitch, species), f32),
            pltpu.VMEM((tiles - 1, pitch, species), f32),
            pltpu.VMEM((pitch * pitch, species), f32),
            pltpu.VMEM((pitch * pitch, species), f32),
            pltpu.VMEM((pitch * pitch, species), f32),
            pltpu.VMEM((nlat * pitch, species), bf16),
            pltpu.VMEM((nlat * pitch, species), bf16),
            pltpu.VMEM((levels, nlat * pitch, species), bf16),
            dma((2,)),
            dma((2,)),
            dma((2,)),
            dma((2,)),
            dma((tiles - 1,)),
            dma((tiles - 1,)),
            dma((tiles - 1,)),
            dma((tiles - 1,)),
            dma((count,)),
            dma((count,)),
            dma,
            dma,
            dma((2, count)),
            dma((2, count)),
        ],
        compiler_params=pltpu.CompilerParams(
            collective_id=0, has_side_effects=True, vmem_limit_bytes=56 * 1024 * 1024
        ),
        name="fused",
    )(*inputs)
    return updated.astype(bf16)[None, None]


def on_device(forcing, *others):
    tiles, levels = lax.axis_size("tile"), lax.axis_size("lev")
    nlon, nlat, species = forcing.shape[2:]
    one_ring = tiles == TJ and levels == 4
    fits = nlon == nlat and nlat % GROUP in (2, 4) and nlat > 3 * GROUP and nlat + 2 * RIM <= 128
    if one_ring and fits and species == 128:
        return on_device_fused(tiles, levels, forcing, *others)
    return on_device_general(forcing, *others)


def solution(mesh):
    in_specs = (
        P("lev", "tile", None, None, None),
        P(None, "lev", "tile", None, None),
        P("lev", "tile", None, None),
        P("lev", None, None),
        P(),
        P("tile", None),
        P("tile", None),
        P(),
        P(),
        P("lev", "tile", None, None, None),
    )
    out_specs = P("lev", "tile", None, None, None)
    return jax.shard_map(
        on_device, mesh=mesh, in_specs=in_specs, out_specs=out_specs, check_vma=False
    )
```

```python
import functools

import jax
import jax.numpy as jnp
from jax import lax
from jax.experimental import pallas as pl
from jax.experimental.pallas import tpu as pltpu
from jax.sharding import PartitionSpec as P

TJ = 8
STEPS = 3


HIGHEST = lax.Precision.HIGHEST


def from_behind(x, axis, by):
    size = lax.axis_size(axis)
    return lax.ppermute(x, axis, [(i, (i + by) % size) for i in range(size)])


def neighbour_rim(edge, offset):
    return from_behind(edge, "tile", offset)


def filter_kernel(rates, blocks):
    cumulative = jnp.cumsum(rates)
    quarter = jnp.sqrt(jnp.sqrt(rates))
    kernel = (
        quarter[:, None]
        * quarter[None, :]
        * jnp.exp(-jnp.abs(cumulative[:, None] - cumulative[None, :]))
    )
    length = rates.shape[0] // blocks
    return kernel.reshape(blocks, length, blocks, length)


def on_device_general(
    forcing,
    transport,
    reactivity,
    jacobian,
    pattern,
    lon_rate,
    lat_rate,
    vertical,
    step_scale,
    control,
):
    adjoint = forcing[0, 0].astype(jnp.float32)
    tile_rows, tile_cols, species = adjoint.shape
    weights = transport[:, 0, 0]
    reacting = reactivity[0, 0][:, :, None]
    groups = pattern.shape[0]
    width = species // groups
    blockmask = jnp.broadcast_to(
        pattern.astype(jnp.float32)[:, None, :, None], (groups, width, groups, width)
    ).reshape(species, species)
    coupling = jacobian[0] * blockmask
    tiles = lax.axis_size("tile")
    lon_tiles = tiles // TJ
    placing = lax.axis_index("tile") % TJ
    keep_south = (placing > 0).astype(jnp.float32)
    keep_north = (placing < TJ - 1).astype(jnp.float32)
    for sweep in range(STEPS):
        if lon_tiles > 1:
            west_rim = neighbour_rim(adjoint[-1], TJ)
            east_rim = neighbour_rim(adjoint[0], -TJ)
        else:
            west_rim = adjoint[-1]
            east_rim = adjoint[0]
        south_rim = neighbour_rim(adjoint[:, -1], 1) * keep_south
        north_rim = neighbour_rim(adjoint[:, 0], -1) * keep_north
        from_west = jnp.concatenate([west_rim[None], adjoint[:-1]], 0)
        from_east = jnp.concatenate([adjoint[1:], east_rim[None]], 0)
        from_south = jnp.concatenate([south_rim[:, None], adjoint[:, :-1]], 1)
        from_north = jnp.concatenate([adjoint[:, 1:], north_rim[:, None]], 1)
        moved = (
            adjoint
            + weights[0][:, :, None] * (from_west - adjoint)
            + weights[1][:, :, None] * (from_east - adjoint)
            + weights[2][:, :, None] * (from_south - adjoint)
            + weights[3][:, :, None] * (from_north - adjoint)
        )
        reacted = jnp.dot(
            moved.reshape(tile_rows * tile_cols, species),
            coupling,
            precision=HIGHEST,
            preferred_element_type=jnp.float32,
        )
        adjoint = moved + reacting * reacted.reshape(tile_rows, tile_cols, species)
    gradient = adjoint.astype(jnp.bfloat16)
    planes = lax.all_to_all(
        gradient.reshape(1, tile_rows * tile_cols, species),
        "tile",
        split_axis=2,
        concat_axis=0,
        tiled=True,
    )
    owned = planes.shape[2]
    planes = jnp.moveaxis(planes.reshape(lon_tiles, TJ, tile_rows, tile_cols, owned), 4, 0)

    def filter_species(inputs):
        lon_line, lat_line, plane = inputs
        lon_kernel = filter_kernel(lon_line, lon_tiles)
        lat_kernel = filter_kernel(lat_line, TJ)
        along_lon = jnp.einsum(
            "abcd,cjdy->ajby", lon_kernel, plane.astype(jnp.float32), precision=HIGHEST
        )
        return jnp.einsum("jykz,akbz->ajby", lat_kernel, along_lon, precision=HIGHEST).astype(
            jnp.bfloat16
        )

    filtered = jnp.moveaxis(lax.map(filter_species, (lon_rate, lat_rate, planes)), 0, 4)
    level_here = lax.axis_index("lev")
    mixing = lax.dynamic_index_in_dim(vertical, level_here, 1, keepdims=False)
    returned = lax.all_to_all(
        filtered.reshape(tiles, tile_rows * tile_cols, owned),
        "tile",
        split_axis=0,
        concat_axis=2,
        tiled=True,
    )
    factor = mixing.T
    summed = jnp.sum(
        lax.all_gather(returned, "lev", axis=0, tiled=True) * factor[:, None, :], axis=0
    )
    increment = summed.reshape(tile_rows, tile_cols, species)
    updated = control[0, 0].astype(jnp.float32) - step_scale * increment
    return updated.astype(jnp.bfloat16)[None, None]


MESH = pl.DeviceIdType.MESH
RIM = STEPS
CHUNK = 10
GROUP = 8


def up_to(size, multiple):
    return -(-size // multiple) * multiple


def fused_kernel(tiles, levels, *refs):
    inputs, out_ref, held, arrived = refs[:10], refs[10], refs[11:21], refs[21]
    (
        forcing_ref,
        transport_ref,
        reactivity_ref,
        jacobian_ref,
        pattern_ref,
        lon_rate_ref,
        lat_rate_ref,
        vertical_ref,
        step_scale_ref,
        control_ref,
    ) = held
    (
        state_a,
        state_b,
        weights_own,
        weights_out,
        weights_rim,
        rim_out,
        rim_in,
        weights,
        moved_ref,
        split_ref,
        plane,
        ahead_ref,
        rates_own,
        rates_all,
        carry_out,
        carry_in,
        plane_far,
        lines_own,
        lines_far,
        grad_out,
        grad_in,
        fields,
        halo_send,
        halo_recv,
        rim_send,
        rim_recv,
        rate_send,
        rate_recv,
        carry_send,
        carry_recv,
        grad_send,
        grad_recv,
        both_send,
        both_recv,
        level_send,
        level_recv,
    ) = refs[22:]
    loads = [
        pltpu.make_async_copy(source, target, arrived.at[k])
        for k, (source, target) in enumerate(zip(inputs, held))
    ]
    for load in loads:
        load.start()
    nlon, nlat, species = forcing_ref.shape
    pitch = state_a.shape[1]
    rows = nlat + 2 * RIM
    rim_rows = rim_out.shape[1]
    owned, lat_total = lat_rate_ref.shape
    lon_at = nlat
    sums_at = nlat + nlon
    rate_width = rates_own.shape[2]
    t = lax.axis_index("tile")
    level = lax.axis_index("lev")
    sibling = level + 1 - 2 * lax.rem(level, 2)
    across = lax.rem(level + 2, levels)
    f32, bf16 = jnp.float32, jnp.bfloat16

    barrier = pltpu.get_barrier_semaphore()
    for o in range(1, tiles):
        pl.semaphore_signal(
            barrier, inc=1, device_id=(level, lax.rem(t + o, tiles)), device_id_type=MESH
        )
    for other in (sibling, across):
        pl.semaphore_signal(barrier, inc=1, device_id=(other, t), device_id_type=MESH)

    weights_own[...] = jnp.zeros_like(weights_own)
    plane[...] = jnp.zeros_like(plane)
    for load in loads[:-1]:
        load.wait()
    weights_own[0:4, 0:nlon, 0:nlat] = transport_ref[...].reshape(4, nlon, nlat)
    weights_own[4, 0:nlon, 0:nlat] = reactivity_ref[...].reshape(nlon, nlat)
    lane = lax.broadcasted_iota(jnp.int32, (pitch, 128), 1)
    thin = RIM - 1
    for side, first in ((0, nlat - thin), (1, 0)):
        packed = jnp.zeros((pitch, 128), f32)
        for d in range(5):
            moved_lanes = pltpu.roll(weights_own[d], (thin * d - first) % 128, 1)
            packed = jnp.where(lane // thin == d, moved_lanes, packed)
        weights_out[side] = packed
    rate_lane = lax.broadcasted_iota(jnp.int32, (owned, rate_width), 1)
    running = jnp.zeros((owned, 1), f32)
    sums_of = jnp.zeros((owned, rate_width), f32)
    for u in range(tiles):
        running = running + jnp.sum(
            lat_rate_ref[:, u * nlat : (u + 1) * nlat], 1, keepdims=True
        )
        sums_of = jnp.where(rate_lane == sums_at + u + 1, running, sums_of)
    for u in range(tiles):
        rates_own[u] = sums_of
        rates_own[u, :, 0:nlat] = lat_rate_ref[:, u * nlat : (u + 1) * nlat]
        rates_own[u, :, lon_at : lon_at + nlon] = lon_rate_ref[...]
    for i in range(nlon):
        plane[i * pitch : i * pitch + nlat, :] = forcing_ref[i].astype(f32)
    plane[nlon * pitch : nlon * pitch + nlat, :] = forcing_ref[0].astype(f32)
    plane[(pitch - 1) * pitch : (pitch - 1) * pitch + nlat, :] = forcing_ref[nlon - 1].astype(f32)
    for j in range(nlat):
        state_a[RIM + j] = plane[pl.ds(j, pitch, stride=pitch), :]
    for side, first in ((0, nlat), (1, RIM)):
        rim_out[side] = jnp.concatenate(
            [
                state_a[first : first + RIM].reshape(RIM * pitch, species),
                jnp.zeros((rim_rows - RIM * pitch, species), f32),
            ],
            0,
        ).astype(bf16)

    pl.semaphore_wait(barrier, tiles + 1)

    def halo(side):
        place = t + 1 - 2 * side
        return (
            pltpu.make_async_remote_copy(
                src_ref=rim_out.at[side],
                dst_ref=rim_in.at[side],
                send_sem=halo_send.at[side],
                recv_sem=halo_recv.at[side],
                device_id=(level, place),
                device_id_type=MESH,
            ),
            pltpu.make_async_remote_copy(
                src_ref=weights_out.at[side],
                dst_ref=weights_rim.at[side],
                send_sem=rim_send.at[side],
                recv_sem=rim_recv.at[side],
                device_id=(level, place),
                device_id_type=MESH,
            ),
        )

    sends = [halo(0), halo(1)]

    @pl.when(t < tiles - 1)
    def _():
        for copy in sends[0]:
            copy.start()

    @pl.when(t > 0)
    def _():
        for copy in sends[1]:
            copy.start()

    @pl.when(t == 0)
    def _():
        rim_in[0] = jnp.zeros(rim_in.shape[1:], bf16)
        weights_rim[0] = jnp.zeros(weights_rim.shape[1:], f32)

    @pl.when(t == tiles - 1)
    def _():
        rim_in[1] = jnp.zeros(rim_in.shape[1:], bf16)
        weights_rim[1] = jnp.zeros(weights_rim.shape[1:], f32)

    mine = pl.ds(pl.multiple_of(t * owned, owned), owned)
    rate_copies = []
    for o in range(1, tiles):
        rate_copies.append(
            pltpu.make_async_remote_copy(
                src_ref=rates_own.at[lax.rem(t + o, tiles)],
                dst_ref=rates_all.at[mine],
                send_sem=rate_send.at[o - 1],
                recv_sem=rate_recv.at[o - 1],
                device_id=(level, lax.rem(t + o, tiles)),
                device_id_type=MESH,
            )
        )
        rate_copies[-1].start()
    rates_all[mine, :] = rates_own[t]

    for j in range(nlat):
        weights[:, RIM + j] = jnp.broadcast_to(
            weights_own[:, :, j : j + 1], (5, pitch, species)
        )

    groups = pattern_ref.shape[0]
    width = species // groups
    member = (
        lax.broadcasted_iota(jnp.int32, (species, groups), 0) // width
        == lax.broadcasted_iota(jnp.int32, (species, groups), 1)
    ).astype(f32)
    mask = lax.dot_general(
        jnp.dot(member, pattern_ref[...].astype(f32), preferred_element_type=f32),
        member,
        (((1,), (1,)), ((), ())),
        preferred_element_type=f32,
    )
    coupling = jacobian_ref[...] * mask
    high = coupling.astype(bf16)
    low = (coupling - high.astype(f32)).astype(bf16)
    both = jnp.concatenate(
        [
            jnp.concatenate([high, low], 1),
            jnp.concatenate([high, jnp.zeros_like(low)], 1),
        ],
        0,
    )

    sums = [jnp.zeros((pitch, species), f32)] * 2

    def step(source, target, first, final, begin, end):
        chunk = GROUP if final else CHUNK
        for j0 in range(begin, end, chunk):
            n = min(chunk, end - j0)
            for j in range(j0, j0 + n, 2):
                here = source[j : j + 2]
                moved = (
                    here
                    + weights[0, j : j + 2] * (pltpu.roll(here, 1, 1) - here)
                    + weights[1, j : j + 2] * (pltpu.roll(here, pitch - 1, 1) - here)
                    + weights[2, j : j + 2] * (source[j - 1 : j + 1] - here)
                    + weights[3, j : j + 2] * (source[j + 1 : j + 3] - here)
                )
                moved = moved.reshape(2 * pitch, species)
                at = pl.ds((j - first) * pitch, 2 * pitch)
                moved_ref[at, :] = moved
                top = moved.astype(bf16)
                split_ref[at, 0:species] = top
                split_ref[at, species:] = (moved - top.astype(f32)).astype(bf16)
            at = pl.ds((j0 - first) * pitch, n * pitch)
            product = jnp.dot(split_ref[at, :], both, preferred_element_type=f32)
            reacted = product[:, :species] + product[:, species:]
            after = moved_ref[at, :].reshape(n, pitch, species) + weights[
                4, j0 : j0 + n
            ] * reacted.reshape(n, pitch, species)
            if final:
                rounded = after.reshape(n * pitch, species).astype(bf16)
                plane[at, :] = rounded.astype(f32)
                exact = rounded.astype(f32)
                packed = [exact[r * pitch : r * pitch + nlon] for r in range(n)]
                grad_out[sent_of((j0 - first) // GROUP), :] = jnp.concatenate(
                    packed, 0
                ).astype(bf16)
                grad_copies[(j0 - first) // GROUP].start()
                for j in range(j0 - first, j0 - first + n):
                    line = rounded[(j - j0 + first) * pitch : (j - j0 + first + 1) * pitch]
                    line = line.astype(f32)
                    sums[0] = sums[0] + to_north[j : j + 1] * line
                    sums[1] = sums[1] + to_south[j : j + 1] * line
            else:
                target[j0 : j0 + n] = after
                target[j0 : j0 + n, nlon : nlon + 1] = after[:, 0:1]
                target[j0 : j0 + n, pitch - 1 : pitch] = after[:, nlon - 1 : nlon]

    groups_at = [(k, min(GROUP, nlat - k)) for k in range(0, nlat, GROUP)]

    def rows_of(k):
        return pl.ds(groups_at[k][0] * pitch, groups_at[k][1] * pitch)

    def sent_of(k):
        return pl.ds(groups_at[k][0] * nlon, groups_at[k][1] * nlon)

    grad_copies = [
        pltpu.make_async_remote_copy(
            src_ref=grad_out.at[sent_of(k)],
            dst_ref=grad_in.at[sent_of(k)],
            send_sem=grad_send.at[k],
            recv_sem=grad_recv.at[k],
            device_id=(across, t),
            device_id_type=MESH,
        )
        for k in range(len(groups_at))
    ]
    spare = pl.ds((nlat + 2) * pitch, (pitch - nlat - 2) * pitch)
    for buffer in (plane, plane_far):
        buffer[spare, :] = jnp.zeros(((pitch - nlat - 2) * pitch, species), f32)
    spare = pl.ds(nlon * pitch, (pitch - nlon) * pitch)
    for buffer in (lines_own, lines_far):
        buffer[spare, :] = jnp.zeros(((pitch - nlon) * pitch, species), f32)

    states = [state_a, state_b]
    low, top = 1, rows - 1
    step(state_a, state_b, low, False, low + RIM + 1, top - RIM - 1)

    @pl.when(t > 0)
    def _():
        sends[0][0].wait_recv()
        sends[0][1].wait_recv()

    @pl.when(t < tiles - 1)
    def _():
        sends[1][0].wait_recv()
        sends[1][1].wait_recv()

    for side, first in ((0, 0), (1, nlat + RIM)):
        rim = rim_in[side].astype(f32)[: RIM * pitch]
        state_a[first : first + RIM] = rim.reshape(RIM, pitch, species)
        for r in range(thin):
            for d in range(5):
                at = thin * d + r
                weights[d, (1, nlat + RIM)[side] + r] = jnp.broadcast_to(
                    weights_rim[side, :, at : at + 1], (pitch, species)
                )

    step(state_a, state_b, low, False, low, low + RIM + 1)
    step(state_a, state_b, low, False, top - RIM - 1, top)

    last_sweep = STEPS - 1
    for sweep in range(1, last_sweep):
        step(
            states[sweep % 2],
            states[(sweep + 1) % 2],
            1 + sweep,
            False,
            1 + sweep,
            rows - 1 - sweep,
        )

    for copy in rate_copies:
        copy.wait()
    cell = lax.broadcasted_iota(jnp.int32, (pitch, rate_width), 1)
    row = lax.broadcasted_iota(jnp.int32, (pitch, rate_width), 0)
    picks = jnp.concatenate(
        [
            (cell == row) & (row < nlat),
            (cell <= row) & (cell < nlat),
            (cell == sums_at + row) & (row <= tiles),
            (cell == lon_at + row) & (row < nlon),
        ],
        0,
    ).astype(f32)
    lines = lax.dot_general(
        picks,
        rates_all[...],
        (((1,), (1,)), ((), ())),
        precision=HIGHEST,
        preferred_element_type=f32,
    )
    lat_line = lines[0:pitch]
    lat_sum = lines[pitch : 2 * pitch]
    before = lines[2 * pitch : 3 * pitch]
    lon_line = lines[3 * pitch :]
    lat_q, lat_d = jnp.sqrt(jnp.sqrt(lat_line)), jnp.exp(-lat_line)
    lon_q, lon_d = jnp.sqrt(jnp.sqrt(lon_line)), jnp.exp(-lon_line)

    to_north = lat_q * jnp.exp(lat_sum - lat_sum[nlat - 1 : nlat])
    to_south = lat_q * jnp.exp(-lat_sum)

    step(
        states[last_sweep % 2],
        None,
        1 + last_sweep,
        True,
        1 + last_sweep,
        rows - 1 - last_sweep,
    )
    carry_out[0] = sums[0]
    carry_out[1] = sums[1]

    carry_copies = []
    for o in range(1, tiles):
        carry_copies.append(
            pltpu.make_async_remote_copy(
                src_ref=carry_out.at[(t + o) // tiles],
                dst_ref=carry_in.at[o - 1],
                send_sem=carry_send.at[o - 1],
                recv_sem=carry_recv.at[o - 1],
                device_id=(level, lax.rem(t + o, tiles)),
                device_id_type=MESH,
            )
        )
        carry_copies[-1].start()

    def along_lon(source, target, first, n):
        def item(i):
            cells = source[pl.ds(first * pitch + i, n, stride=pitch), :]
            return lon_q[i : i + 1] * cells

        carry = jnp.zeros((n, species), f32)
        for i in range(nlon):
            carry = item(i) + lon_d[i : i + 1] * carry
            target[pl.ds(i * pitch + first, n), :] = carry
        later = jnp.zeros((n, species), f32)
        for i in range(nlon - 1, -1, -1):
            at = pl.ds(i * pitch + first, n)
            target[at, :] = lon_q[i : i + 1] * (target[at, :] + later)
            later = lon_d[i : i + 1] * (item(i) + later)

    def take(k):
        grad_copies[k].wait_recv()
        first, n = groups_at[k]
        cells = grad_in[sent_of(k), :].astype(f32)
        for r in range(n):
            plane_far[pl.ds((first + r) * pitch, nlon), :] = cells[r * nlon : (r + 1) * nlon]

    split_at = len(groups_at) - 2
    along_lon(plane, lines_own, 0, (len(groups_at) - 1) * GROUP)
    for begin, end in ((0, split_at - 1), (split_at - 1, split_at)):
        for k in range(begin, end):
            take(k)
        along_lon(plane_far, lines_far, begin * GROUP, (end - begin) * GROUP)

    order = lax.broadcasted_iota(jnp.int32, (pitch, species), 0)

    def before_tile(u):
        return jnp.sum(jnp.where(order == u, before, 0.0), 0, keepdims=True)

    south = jnp.zeros((pitch, species), f32)
    north = jnp.zeros((pitch, species), f32)
    for o in range(1, tiles):
        u = lax.rem(t + tiles - o, tiles)
        upper, lower = jnp.maximum(u, t), jnp.minimum(u, t)
        factor = jnp.exp(before_tile(lower + 1) - before_tile(upper))
        carry_copies[o - 1].wait()
        term = factor * carry_in[o - 1]
        south = south + jnp.where(o <= t, term, 0.0)
        north = north + jnp.where(o <= t, 0.0, term)
    plane[nlat * pitch : (nlat + 1) * pitch, :] = south
    plane[(nlat + 1) * pitch : (nlat + 2) * pitch, :] = north
    carried = pl.ds(nlat * pitch, 2 * pitch)
    both_copy = pltpu.make_async_remote_copy(
        src_ref=plane.at[carried],
        dst_ref=plane_far.at[carried],
        send_sem=both_send,
        recv_sem=both_recv,
        device_id=(across, t),
        device_id_type=MESH,
    )
    both_copy.start()

    def along_lat(lines_ref, slot):
        def line(j):
            return lines_ref[pl.ds(j, pitch, stride=pitch), :]

        carry = line(nlat)
        for j in range(nlat):
            carry = lat_q[j : j + 1] * line(j) + lat_d[j : j + 1] * carry
            ahead_ref[j] = carry
        later = line(nlat + 1)
        copies = {}
        for k in range(len(groups_at) - 1, -1, -1):
            first, n = groups_at[k]
            for j in range(first + n - 2, first - 1, -2):
                done = []
                for row_at in (j + 1, j):
                    q = lat_q[row_at : row_at + 1]
                    done.append(q * (ahead_ref[row_at] + later))
                    later = lat_d[row_at : row_at + 1] * (q * line(row_at) + later)
                fields[slot, pl.ds(j * pitch, 2 * pitch), :] = jnp.concatenate(
                    done[::-1], 0
                ).astype(bf16)
            copies[k] = pltpu.make_async_remote_copy(
                src_ref=fields.at[slot, rows_of(k)],
                dst_ref=fields.at[slot + 1, rows_of(k)],
                send_sem=level_send.at[slot // 2, k],
                recv_sem=level_recv.at[slot // 2, k],
                device_id=(sibling, t),
                device_id_type=MESH,
            )
            copies[k].start()
        return copies

    last_group = len(groups_at) - 1
    along_lon(plane, lines_own, last_group * GROUP, pitch - last_group * GROUP)
    near = along_lat(lines_own, 0)
    for k in range(split_at, len(groups_at)):
        take(k)
    both_copy.wait_recv()
    along_lon(plane_far, lines_far, split_at * GROUP, pitch - split_at * GROUP)
    relay = along_lat(lines_far, 2)

    loads[-1].wait()
    factors = [
        vertical_ref[level, pl.ds(source, 1), :]
        for source in (level, sibling, across, lax.rem(sibling + 2, levels))
    ]
    scale = step_scale_ref[...]
    for k in range(last_group, -1, -1):
        near[k].wait_recv()
        relay[k].wait_recv()
        at = rows_of(k)
        total = factors[0] * fields[0, at, :].astype(f32)
        for slot in range(1, levels):
            total = total + factors[slot] * fields[slot, at, :].astype(f32)
        moved_ref[at, :] = scale * total
    for i in range(nlon):
        total = moved_ref[pl.ds(i, pitch, stride=pitch), :]
        out_ref[i] = (control_ref[i].astype(f32) - total[:nlat]).astype(bf16)
    @pl.when(t < tiles - 1)
    def _():
        sends[0][0].wait_send()
        sends[0][1].wait_send()

    @pl.when(t > 0)
    def _():
        sends[1][0].wait_send()
        sends[1][1].wait_send()

    both_copy.wait_send()
    for k in range(len(groups_at)):
        grad_copies[k].wait_send()
        near[k].wait_send()
        relay[k].wait_send()


def on_device_fused(
    tiles,
    levels,
    forcing,
    transport,
    reactivity,
    jacobian,
    pattern,
    lon_rate,
    lat_rate,
    vertical,
    step_scale,
    control,
):
    nlon, nlat, species = forcing.shape[2:]
    pitch = up_to(max(nlon + 2, nlat), 8)
    rows = nlat + 2 * RIM
    owned, lat_total = lat_rate.shape
    rate_width = up_to(nlat + nlon + tiles + 1, 128)
    f32, bf16 = jnp.float32, jnp.bfloat16
    dma = pltpu.SemaphoreType.DMA
    count = -(-nlat // GROUP)
    rim_rows = up_to(RIM * pitch, 16)
    inputs = (
        forcing[0, 0],
        transport[:, 0, 0][:, :, None],
        reactivity[0, 0][:, None],
        jacobian[0],
        pattern,
        lon_rate,
        lat_rate,
        jnp.transpose(vertical, (1, 2, 0)),
        step_scale[None],
        control[0, 0],
    )
    updated = pl.pallas_call(
        functools.partial(fused_kernel, tiles, levels),
        out_shape=jax.ShapeDtypeStruct((nlon, nlat, species), bf16),
        in_specs=[pl.BlockSpec(memory_space=pltpu.HBM)] * 10,
        out_specs=pl.BlockSpec(memory_space=pltpu.VMEM),
        scratch_shapes=[pltpu.VMEM(x.shape, x.dtype) for x in inputs]
        + [
            dma((len(inputs),)),
            pltpu.VMEM((rows, pitch, species), f32),
            pltpu.VMEM((rows, pitch, species), f32),
            pltpu.VMEM((5, pitch, 128), f32),
            pltpu.VMEM((2, pitch, 128), f32),
            pltpu.VMEM((2, pitch, 128), f32),
            pltpu.VMEM((2, rim_rows, species), bf16),
            pltpu.VMEM((2, rim_rows, species), bf16),
            pltpu.VMEM((5, rows, pitch, species), f32),
            pltpu.VMEM((rows * pitch, species), f32),
            pltpu.VMEM((rows * pitch, 2 * species), bf16),
            pltpu.VMEM((pitch * pitch, species), f32),
            pltpu.VMEM((pitch, pitch, species), f32),
            pltpu.VMEM((tiles, owned, rate_width), f32),
            pltpu.VMEM((species, rate_width), f32),
            pltpu.VMEM((2, pitch, species), f32),
            pltpu.VMEM((tiles - 1, pitch, species), f32),
            pltpu.VMEM((pitch * pitch, species), f32),
            pltpu.VMEM((pitch * pitch, species), f32),
            pltpu.VMEM((pitch * pitch, species), f32),
            pltpu.VMEM((nlat * nlon, species), bf16),
            pltpu.VMEM((nlat * nlon, species), bf16),
            pltpu.VMEM((levels, nlat * pitch, species), bf16),
            dma((2,)),
            dma((2,)),
            dma((2,)),
            dma((2,)),
            dma((tiles - 1,)),
            dma((tiles - 1,)),
            dma((tiles - 1,)),
            dma((tiles - 1,)),
            dma((count,)),
            dma((count,)),
            dma,
            dma,
            dma((2, count)),
            dma((2, count)),
        ],
        compiler_params=pltpu.CompilerParams(
            collective_id=0, has_side_effects=True, vmem_limit_bytes=56 * 1024 * 1024
        ),
        name="fused",
    )(*inputs)
    return updated[None, None]


def on_device(forcing, *others):
    tiles, levels = lax.axis_size("tile"), lax.axis_size("lev")
    nlon, nlat, species = forcing.shape[2:]
    one_ring = tiles == TJ and levels == 4
    fits = nlon == nlat and nlat % GROUP in (2, 4) and nlat > 3 * GROUP and nlat * nlon % 16 == 0 and nlat + 2 * RIM <= 128
    if one_ring and fits and species == 128:
        return on_device_fused(tiles, levels, forcing, *others)
    return on_device_general(forcing, *others)


def solution(mesh):
    in_specs = (
        P("lev", "tile", None, None, None),
        P(None, "lev", "tile", None, None),
        P("lev", "tile", None, None),
        P("lev", None, None),
        P(),
        P("tile", None),
        P("tile", None),
        P(),
        P(),
        P("lev", "tile", None, None, None),
    )
    out_specs = P("lev", "tile", None, None, None)
    return jax.shard_map(
        on_device, mesh=mesh, in_specs=in_specs, out_specs=out_specs, check_vma=False
    )
```
